32 devices in a mesh: smp: 4 (over x, core), ctx: 8 (over z, y).
Axes of the slice: x: 2, y: 2, z: 4, core: 2. Of those that a mesh axis runs over, the one named last changes fastest.
Arguments:
- query: bfloat16 [4, 1024, 4096], P('smp', 'ctx'), may hold values from -6 to 6
- d_out: bfloat16 [4, 1024, 4096], P('smp', 'ctx'), may hold values from -6 to 6
- branch_kv: bfloat16 [4, 1024, 1024], P('smp', 'ctx'), may hold values from -6 to 6
- prefix_kv: bfloat16 [256, 1024], P('ctx', 'smp'), may hold values from -6 to 6
- parents: int32 [4, 8], P('smp'), may hold values from -1 to 6, as said below
- lengths: int32 [4, 8], P('smp'), may hold values from 33 to 128, as said below
Outputs:
- attn_out: bfloat16 [4, 1024, 4096], P('smp', 'ctx')
- d_query: bfloat16 [4, 1024, 4096], P('smp', 'ctx')
- d_branch_kv: bfloat16 [4, 1024, 1024], P('smp', 'ctx')
- d_prefix_kv: bfloat16 [256, 1024], P('ctx', 'smp')
The draws below stay inside these ranges and needn't reach their ends.
Inputs may be any that keep to these rules, and one draw needn't show every extreme that they name: parents[s, 0] = -1; for i > 0 parents[s, i] lies below i; every path from the prefix to a block has at most 4 blocks, the block included, and block 3 of every sample has exactly 4; parents[s, 7] = 6. lengths[s, 0] = 128 and lengths[s, 1] = 33.
All inputs are finite; a program needn't handle non-finite values.
Results may differ from the reference program's by a relative error of at most 0.03.
Values may be sent and summed in bfloat16 or wider, within the bound.
A program may use at most 128 MiB of HBM per device.

```python
import jax
import jax.numpy as jnp
from jax import lax

HQ = 32
HK = 4
HD = 128
FEAT = 1024
BLOCK = 128
PREFIX = 256
NB = 8
BTOK = 1024
DEPTH = 4
SAMPLES = 4


def draw_prefix_kv(key, part):
    key = jax.random.fold_in(key, 11)
    base_draw = jnp.clip(jax.random.normal(key, (PREFIX, FEAT), jnp.float32), -6.0, 6.0)
    return base_draw.astype(jnp.bfloat16)


def draw_query(key, part):
    key = jax.random.fold_in(key, 13)
    base_draw = jnp.clip(jax.random.normal(key, (SAMPLES, BTOK, HQ * HD), jnp.float32), -6.0, 6.0)
    return base_draw.astype(jnp.bfloat16)


def draw_parents(key, part):
    key = jax.random.fold_in(key, 5)
    coin_key, target_key = jax.random.split(key)
    coins = jax.random.randint(coin_key, (SAMPLES, NB), 0, 2, dtype=jnp.int32)
    jump_target = jax.random.randint(target_key, (SAMPLES, NB), 0, DEPTH - 1, dtype=jnp.int32)
    path_limit = DEPTH

    def one_sample(inputs):
        coin_row, jump_row = inputs

        def scan_step(path_depth, step_inputs):
            index, coin, target = step_inputs
            chain = index < path_limit
            force_jump = index == NB - 2
            force_grow = index == NB - 1
            target = jnp.where(force_jump, jnp.minimum(target, path_limit - 3), target)
            grows = chain | force_grow | jnp.logical_not(force_jump) & (path_depth < path_limit) & (coin == 1)
            parent = jnp.where(index == 0, -1, jnp.where(grows, index - 1, target))
            new_depth = jnp.where(index == 0, 1, jnp.where(grows, path_depth + 1, target + 2))
            return (new_depth.astype(jnp.int32), parent.astype(jnp.int32))
        _, parent_row = lax.scan(scan_step, jnp.int32(0), (jnp.arange(NB, dtype=jnp.int32), coin_row, jump_row))
        return parent_row
    return jax.vmap(one_sample)((coins, jump_target))


def draw_lengths(key, part):
    key = jax.random.fold_in(key, 7)
    drawn = BLOCK // 4 + 1 + jax.random.randint(key, (SAMPLES, NB), 0, BLOCK - BLOCK // 4, dtype=jnp.int32)
    drawn = drawn.at[:, 0].set(BLOCK)
    drawn = drawn.at[:, 1].set(BLOCK // 4 + 1)
    return drawn


def levels(rng, shape, cuts, low, top_value):
    def one(dim, parts):
        draws = jax.random.uniform(jax.random.fold_in(jax.random.fold_in(rng, 6), dim), (parts,), jnp.float32, low / len(cuts), top_value / len(cuts))
        return jnp.repeat(jnp.exp(draws), shape[dim] // parts).reshape((-1,) + (1,) * (len(shape) - dim - 1))

    factor_of = one(*cuts[0])
    for cut in cuts[1:]:
        factor_of = factor_of * one(*cut)
    return factor_of


def centred(rng, dims, spread, limit, cuts=(), held_as=jnp.bfloat16):
    level = levels(rng, dims, cuts, -0.22, 0.18) if cuts else 1.0
    values = jax.random.normal(rng, dims, jnp.float32) * spread * level
    return jnp.minimum(jnp.maximum(values, -limit), limit).astype(held_as)


def setup_inputs(seed: int = 0) -> dict:
    seeds = jax.random.split(jax.random.key(seed), 7)
    query = draw_query(jax.random.fold_in(seeds[6], 71), 0)
    d_out = centred(seeds[1], (SAMPLES, BTOK, HQ * HD), 1.0, 6.0, ((0, 4), (1, 8)))
    branch_kv = centred(seeds[2], (SAMPLES, BTOK, FEAT), 1.0, 6.0, ((0, 4), (1, 8)))
    prefix_kv = draw_prefix_kv(jax.random.fold_in(seeds[6], 71), 0)
    parents = draw_parents(jax.random.fold_in(seeds[6], 71), 0)
    lengths = draw_lengths(jax.random.fold_in(seeds[6], 71), 0)
    return {"query": query, "d_out": d_out, "branch_kv": branch_kv, "prefix_kv": prefix_kv, "parents": parents, "lengths": lengths}


def build_masks(parent_row, length_row, block_index, depth_slots, block_rows, prefix_rows):
    num_blocks = parent_row.shape[0]
    indices = jnp.arange(num_blocks, dtype=jnp.int32)
    parent_links = (parent_row[:, None] == indices[None, :]).astype(jnp.float32)
    reachable = jnp.eye(num_blocks, dtype=jnp.float32) + parent_links
    for _ in range(num_blocks.bit_length()):
        reachable = jnp.minimum(jnp.dot(reachable, reachable, precision=lax.Precision.HIGHEST), 1.0)
    pick_row = (indices == block_index).astype(jnp.float32)
    ancestry = jnp.dot(pick_row, reachable, precision=lax.Precision.HIGHEST)
    position = jnp.cumsum(ancestry) - 1.0
    slot_ids = jnp.arange(depth_slots, dtype=jnp.float32)
    selector = ancestry[None, :] * (position[None, :] == slot_ids[:, None]).astype(jnp.float32)
    block_float = indices.astype(jnp.float32)
    owner_block = jnp.dot(selector, block_float, precision=lax.Precision.HIGHEST)
    slot_used = jnp.sum(selector, axis=1) > 0.5
    own_slot = slot_used & (jnp.abs(owner_block - jnp.sum(pick_row * block_float)) < 0.5)
    lengths_float = length_row.astype(jnp.float32)
    slot_length = jnp.dot(selector, lengths_float, precision=lax.Precision.HIGHEST)
    own_length = jnp.sum(pick_row * lengths_float)
    place = jnp.arange(block_rows, dtype=jnp.float32)
    row_place = place[:, None, None]
    key_place = place[None, None, :]
    slot_allowed = slot_used[None, :, None] & (key_place < slot_length[None, :, None]) & (
        jnp.logical_not(own_slot)[None, :, None] | (key_place <= row_place))
    key_allowed = jnp.concatenate(
        [jnp.ones((block_rows, prefix_rows), dtype=jnp.bool_),
         slot_allowed.reshape(block_rows, depth_slots * block_rows)], axis=1)
    row_valid = place < own_length
    return selector, key_allowed, row_valid


def attend(query_block, dout_block, key_values, key_allowed, row_valid, heads_kv, head_dim):
    row_count = query_block.shape[0]
    query_width = query_block.shape[1]
    group_size = query_width // (heads_kv * head_dim)
    key_count = key_values.shape[0]
    softmax_scale = head_dim ** -0.5
    grad_live = jnp.where(row_valid[:, None], dout_block, jnp.zeros_like(dout_block))
    query_heads = query_block.reshape(row_count, heads_kv, group_size, head_dim).transpose(1, 0, 2, 3).reshape(
        heads_kv, row_count * group_size, head_dim)
    grad_heads = grad_live.reshape(row_count, heads_kv, group_size, head_dim).transpose(1, 0, 2, 3).reshape(
        heads_kv, row_count * group_size, head_dim)
    key_heads = key_values[:, : heads_kv * head_dim].reshape(key_count, heads_kv, head_dim).transpose(1, 0, 2)
    value_heads = key_values[:, heads_kv * head_dim:].reshape(key_count, heads_kv, head_dim).transpose(1, 0, 2)
    mask_rows = jnp.repeat(key_allowed, group_size, axis=0)
    live_rows = jnp.repeat(row_valid, group_size)

    def one_head(inputs):
        query_head, grad_head, key_head, value_head = inputs
        scores = jnp.dot(query_head, key_head.T, preferred_element_type=jnp.float32) * softmax_scale
        scores = jnp.where(mask_rows, scores, -jnp.inf)
        row_max = jnp.max(scores, axis=1, keepdims=True)
        exponent = jnp.exp(scores - row_max)
        probability = exponent / jnp.sum(exponent, axis=1, keepdims=True)
        prob_round = probability.astype(jnp.bfloat16)
        attended = jnp.dot(prob_round, value_head, preferred_element_type=jnp.float32)
        attended_out = jnp.where(live_rows[:, None], attended, 0.0).astype(jnp.bfloat16)
        grad_probs = jnp.dot(grad_head, value_head.T, preferred_element_type=jnp.float32)
        row_delta = jnp.sum(grad_head.astype(jnp.float32) * attended_out.astype(jnp.float32), axis=1, keepdims=True)
        grad_scores = (probability * (grad_probs - row_delta)).astype(jnp.bfloat16)
        grad_query = (jnp.dot(grad_scores, key_head, preferred_element_type=jnp.float32) * softmax_scale).astype(jnp.bfloat16)
        grad_keys = jnp.dot(grad_scores.T, query_head, preferred_element_type=jnp.float32) * softmax_scale
        grad_values = jnp.dot(prob_round.T, grad_head, preferred_element_type=jnp.float32)
        return attended_out, grad_query, grad_keys, grad_values

    attended_all, grad_query_all, grad_keys_all, grad_values_all = lax.map(
        one_head, (query_heads, grad_heads, key_heads, value_heads))
    output = attended_all.reshape(heads_kv, row_count, group_size, head_dim).transpose(1, 0, 2, 3).reshape(row_count, query_width)
    grad_query_out = grad_query_all.reshape(heads_kv, row_count, group_size, head_dim).transpose(1, 0, 2, 3).reshape(row_count, query_width)
    grad_pairs = jnp.concatenate(
        [grad_keys_all.transpose(1, 0, 2).reshape(key_count, heads_kv * head_dim),
         grad_values_all.transpose(1, 0, 2).reshape(key_count, heads_kv * head_dim)], axis=1)
    return output, grad_query_out, grad_pairs


def reference(query, d_out, branch_kv, prefix_kv, parents, lengths):
    def one_sample(inputs):
        query_sample, dout_sample, pairs_sample, parent_row, length_row = inputs
        blocks_kv = pairs_sample.reshape(NB, BLOCK, FEAT)

        def scan_step(totals, block_index):
            grad_blocks, grad_prefix = totals
            start_row = (block_index * BLOCK).astype(jnp.int32)
            query_block = lax.dynamic_slice_in_dim(query_sample, start_row, BLOCK, 0)
            dout_block = lax.dynamic_slice_in_dim(dout_sample, start_row, BLOCK, 0)
            selector, key_allowed, row_valid = build_masks(parent_row, length_row, block_index, DEPTH, BLOCK, PREFIX)
            picked = jnp.einsum("kn,nbf->kbf", selector, blocks_kv.astype(jnp.float32),
                                precision=lax.Precision.HIGHEST).astype(jnp.bfloat16)
            key_values = jnp.concatenate([prefix_kv, picked.reshape(DEPTH * BLOCK, FEAT)], axis=0)
            output, grad_query, grad_pairs = attend(query_block, dout_block, key_values, key_allowed, row_valid, HK, HD)
            grad_prefix = grad_prefix + grad_pairs[:PREFIX]
            slot_grads = grad_pairs[PREFIX:].reshape(DEPTH, BLOCK, FEAT)
            grad_blocks = grad_blocks + jnp.einsum("kn,kbf->nbf", selector, slot_grads, precision=lax.Precision.HIGHEST)
            return (grad_blocks, grad_prefix), (output, grad_query)

        initial = (jnp.zeros((NB, BLOCK, FEAT), jnp.float32), jnp.zeros((PREFIX, FEAT), jnp.float32))
        (grad_blocks, grad_prefix), (outputs, grad_queries) = lax.scan(
            scan_step, initial, jnp.arange(NB, dtype=jnp.int32))
        return (outputs.reshape(BTOK, HQ * HD), grad_queries.reshape(BTOK, HQ * HD),
                grad_blocks.reshape(BTOK, FEAT), grad_prefix)

    outputs, grad_queries, grad_branch, grad_prefix = lax.map(
        one_sample, (query, d_out, branch_kv, parents, lengths))
    return outputs, grad_queries, grad_branch.astype(jnp.bfloat16), jnp.sum(grad_prefix, axis=0).astype(jnp.bfloat16)
```

```python
import functools
import math

import jax
import jax.numpy as jnp
from jax import lax
from jax.experimental import pallas as pl
from jax.experimental.pallas import tpu as pltpu
from jax.sharding import PartitionSpec as P

HK = 4
HD = 128
F32 = jnp.float32
BF16 = jnp.bfloat16


def walk_up(parents, lengths, start, count):
    found = []
    at = start
    for _ in range(count):
        up = parents[0, jnp.maximum(at, 0)]
        at = jnp.where(at >= 0, up, -1)
        held = jnp.maximum(at, 0)
        found.append((held, jnp.where(at >= 0, lengths[0, held], 0), at >= 0))
    return found


def attend_group(query, d_out, keys, values, prefix_rows, own_length, slot_lengths):
    block = query.shape[0]
    group = query.shape[1] // HD
    scale = HD ** -0.5
    to_exp2 = scale * math.log2(math.e)
    place = lax.broadcasted_iota(jnp.int32, (block, 1), 0)
    grad_live = jnp.where(place < own_length, d_out, jnp.zeros_like(d_out))

    def heads(x):
        return [x[:, h * HD:(h + 1) * HD] for h in range(group)]

    query_rows = jnp.concatenate(heads(query), axis=0)
    grad_rows = jnp.concatenate(heads(grad_live), axis=0)
    grad_cols = jnp.concatenate([h.T for h in heads(grad_live)], axis=1)

    scores = lax.dot_general(keys, query_rows, (((1,), (1,)), ((), ())), preferred_element_type=F32)
    row = lax.broadcasted_iota(jnp.int32, (block, block), 1)
    key = lax.broadcasted_iota(jnp.int32, (block, block), 0)
    own_bias = jnp.where((key < own_length) & (key <= row), 0.0, -jnp.inf)
    own_bias = jnp.concatenate([own_bias] * group, axis=1)
    parts = [scores[:prefix_rows], scores[prefix_rows:prefix_rows + block] + own_bias]
    for s, length in enumerate(slot_lengths):
        first = prefix_rows + (s + 1) * block
        parts.append(scores[first:first + block] + jnp.where(place < length, 0.0, -jnp.inf))
    scores = jnp.concatenate(parts, axis=0)
    top = jnp.max(scores, axis=0, keepdims=True) * to_exp2
    exponent = jnp.exp2(scores * to_exp2 - top)
    probs = exponent * (1.0 / jnp.sum(exponent, axis=0, keepdims=True))
    probs_low = probs.astype(BF16)
    attended = lax.dot_general(values, probs_low, (((0,), (0,)), ((), ())), preferred_element_type=F32)
    live = lax.broadcasted_iota(jnp.int32, (1, block), 1) < own_length
    live = jnp.concatenate([jnp.where(live, 1.0, 0.0)] * group, axis=1)
    attended = (attended * live).astype(BF16)
    delta = jnp.sum(grad_cols.astype(F32) * attended.astype(F32), axis=0, keepdims=True)
    grad_probs = jnp.dot(values, grad_cols, preferred_element_type=F32)
    grad_scores = (probs * (grad_probs - delta)).astype(BF16)
    grad_query = lax.dot_general(keys, grad_scores, (((0,), (0,)), ((), ())), preferred_element_type=F32)
    grad_query = (grad_query * scale).astype(BF16)
    grad_keys = jnp.dot(grad_scores, query_rows, preferred_element_type=F32) * scale
    grad_values = jnp.dot(probs_low, grad_rows, preferred_element_type=F32)
    return (
        jnp.concatenate([h.T for h in heads_across(attended, block)], axis=1),
        jnp.concatenate([h.T for h in heads_across(grad_query, block)], axis=1),
        grad_keys,
        grad_values,
    )


def heads_across(x, block):
    return [x[:, h * block:(h + 1) * block] for h in range(x.shape[1] // block)]


def attend_kernel(
    slots, parents, lengths, query, d_out, prefix_k, prefix_v, branch_k, branch_v,
    out, d_query, d_prefix_k, d_prefix_v, d_branch_k, d_branch_v,
):
    me = lax.axis_index("ctx")
    prefix_rows = prefix_k.shape[0]
    block = query.shape[0]
    found = walk_up(parents, lengths, me, slots)
    blocks = [me] + [index for index, _, _ in found]
    keys = jnp.concatenate([prefix_k[...]] + [branch_k[b] for b in blocks], axis=0)
    values = jnp.concatenate([prefix_v[...]] + [branch_v[b] for b in blocks], axis=0)
    out[...], d_query[...], grad_keys, grad_values = attend_group(
        query[...], d_out[...], keys, values, prefix_rows, lengths[0, me], [length for _, length, _ in found]
    )
    for grads, to_prefix, to_branch in ((grad_keys, d_prefix_k, d_branch_k), (grad_values, d_prefix_v, d_branch_v)):
        to_prefix[...] = grads[:prefix_rows]
        to_branch[...] = jnp.zeros_like(to_branch)
        for s, b in enumerate(blocks):
            first = prefix_rows + s * block
            piece = grads[first:first + block]
            if s == 0:
                to_branch[b] = piece
            else:
                @pl.when(found[s - 1][2])
                def _():
                    to_branch[b] = piece


def per_device(query, d_out, branch_kv, prefix_kv, parents, lengths):
    num_blocks = parents.shape[1]
    slots = max(4, num_blocks // 4) - 1
    block = query.shape[1]
    width = query.shape[2]
    with_features = lax.all_gather(prefix_kv, "smp", axis=1, tiled=True)
    prefix_all = lax.all_gather(with_features, "ctx", axis=0, tiled=True)
    prefix_rows, features = prefix_all.shape
    all_blocks = lax.all_gather(branch_kv[0], "ctx", axis=0)
    group_width = width // HK
    smem = pl.BlockSpec(memory_space=pltpu.SMEM)
    heads = pl.BlockSpec((block, group_width), lambda g: (0, g))
    prefix_k = pl.BlockSpec((prefix_rows, HD), lambda g: (0, g))
    prefix_v = pl.BlockSpec((prefix_rows, HD), lambda g: (0, g + HK))
    branch_k = pl.BlockSpec((num_blocks, block, HD), lambda g: (0, 0, g))
    branch_v = pl.BlockSpec((num_blocks, block, HD), lambda g: (0, 0, g + HK))
    grad_prefix = jax.ShapeDtypeStruct((prefix_rows, features // 2), F32)
    grad_branch = jax.ShapeDtypeStruct((num_blocks, block, features // 2), F32)
    out, d_query, dpk, dpv, dbk, dbv = pl.pallas_call(
        functools.partial(attend_kernel, slots),
        grid=(HK,),
        in_specs=[smem, smem, heads, heads, prefix_k, prefix_v, branch_k, branch_v],
        out_specs=[heads, heads, prefix_k, prefix_k, branch_k, branch_k],
        out_shape=[
            jax.ShapeDtypeStruct((block, width), BF16),
            jax.ShapeDtypeStruct((block, width), BF16),
            grad_prefix, grad_prefix, grad_branch, grad_branch,
        ],
        compiler_params=pltpu.CompilerParams(vmem_limit_bytes=56 * 1024 * 1024),
    )(parents, lengths, query[0], d_out[0], prefix_all, prefix_all, all_blocks, all_blocks)
    spread = jnp.concatenate([dbk, dbv], axis=2).reshape(num_blocks * block, features)
    grad_branch = lax.psum_scatter(spread, "ctx", scatter_dimension=0, tiled=True)
    grad_rows = lax.psum_scatter(jnp.concatenate([dpk, dpv], axis=1), "ctx", scatter_dimension=0, tiled=True)
    grad_prefix_out = lax.psum_scatter(grad_rows, "smp", scatter_dimension=1, tiled=True)
    return out[None], d_query[None], grad_branch.astype(BF16)[None], grad_prefix_out.astype(BF16)


def solution(mesh):
    return jax.shard_map(
        per_device,
        mesh=mesh,
        in_specs=(
            P("smp", "ctx", None),
            P("smp", "ctx", None),
            P("smp", "ctx", None),
            P("ctx", "smp"),
            P("smp", None),
            P("smp", None),
        ),
        out_specs=(
            P("smp", "ctx", None),
            P("smp", "ctx", None),
            P("smp", "ctx", None),
            P("ctx", "smp"),
        ),
        check_vma=False,
    )
```

```python
import functools
import math

import jax
import jax.numpy as jnp
from jax import lax
from jax.experimental import pallas as pl
from jax.experimental.pallas import tpu as pltpu
from jax.sharding import PartitionSpec as P

HK = 4
HD = 128
F32 = jnp.float32
BF16 = jnp.bfloat16


def walk_up(parents, lengths, start, count):
    found = []
    at = start
    for _ in range(count):
        up = parents[0, jnp.maximum(at, 0)]
        at = jnp.where(at >= 0, up, -1)
        held = jnp.maximum(at, 0)
        found.append((held, jnp.where(at >= 0, lengths[0, held], 0), at >= 0))
    return found


def attend_group(query, d_out, keys, values, prefix_rows, own_length, slot_lengths):
    block = query.shape[0]
    group = query.shape[1] // HD
    scale = HD ** -0.5
    to_exp2 = scale * math.log2(math.e)
    place = lax.broadcasted_iota(jnp.int32, (block, 1), 0)
    grad_live = jnp.where(place < own_length, d_out, jnp.zeros_like(d_out))

    def heads(x):
        return [x[:, h * HD:(h + 1) * HD] for h in range(group)]

    query_rows = jnp.concatenate(heads(query), axis=0)
    grad_rows = jnp.concatenate(heads(grad_live), axis=0)
    grad_cols = jnp.concatenate([h.T for h in heads(grad_live)], axis=1)

    scores = lax.dot_general(keys, query_rows, (((1,), (1,)), ((), ())), preferred_element_type=F32)
    row = lax.broadcasted_iota(jnp.int32, (block, block), 1)
    key = lax.broadcasted_iota(jnp.int32, (block, block), 0)
    own_bias = jnp.where((key < own_length) & (key <= row), 0.0, -jnp.inf)
    own_bias = jnp.concatenate([own_bias] * group, axis=1)
    parts = [scores[:prefix_rows], scores[prefix_rows:prefix_rows + block] + own_bias]
    for s, length in enumerate(slot_lengths):
        first = prefix_rows + (s + 1) * block
        parts.append(scores[first:first + block] + jnp.where(place < length, 0.0, -jnp.inf))
    scores = jnp.concatenate(parts, axis=0)
    top = jnp.max(scores, axis=0, keepdims=True) * to_exp2
    exponent = jnp.exp2(scores * to_exp2 - top)
    probs = exponent * (1.0 / jnp.sum(exponent, axis=0, keepdims=True))
    probs_low = probs.astype(BF16)
    attended = lax.dot_general(values, probs_low, (((0,), (0,)), ((), ())), preferred_element_type=F32)
    live = lax.broadcasted_iota(jnp.int32, (1, block), 1) < own_length
    live = jnp.concatenate([jnp.where(live, 1.0, 0.0)] * group, axis=1)
    attended = (attended * live).astype(BF16)
    delta = jnp.sum(grad_cols.astype(F32) * attended.astype(F32), axis=0, keepdims=True)
    grad_probs = jnp.dot(values, grad_cols, preferred_element_type=F32)
    grad_scores = (probs * (grad_probs - delta)).astype(BF16)
    grad_query = lax.dot_general(keys, grad_scores, (((0,), (0,)), ((), ())), preferred_element_type=F32)
    grad_query = (grad_query * scale).astype(BF16)
    grad_keys = jnp.dot(grad_scores, query_rows, preferred_element_type=F32) * scale
    grad_values = jnp.dot(probs_low, grad_rows, preferred_element_type=F32)
    return (
        jnp.concatenate([h.T for h in heads_across(attended, block)], axis=1),
        jnp.concatenate([h.T for h in heads_across(grad_query, block)], axis=1),
        grad_keys,
        grad_values,
    )


def heads_across(x, block):
    return [x[:, h * block:(h + 1) * block] for h in range(x.shape[1] // block)]


def attend_kernel(
    slots, parents, lengths, query, d_out, prefix_k, prefix_v, branch_k, branch_v,
    out, d_query, d_prefix_k, d_prefix_v, d_branch_k, d_branch_v,
):
    me = lax.axis_index("ctx")
    prefix_rows = prefix_k.shape[0]
    block = query.shape[0]
    found = walk_up(parents, lengths, me, slots)
    blocks = [me] + [index for index, _, _ in found]
    keys = jnp.concatenate([prefix_k[...]] + [branch_k[b] for b in blocks], axis=0)
    values = jnp.concatenate([prefix_v[...]] + [branch_v[b] for b in blocks], axis=0)
    out[...], d_query[...], grad_keys, grad_values = attend_group(
        query[...], d_out[...], keys, values, prefix_rows, lengths[0, me], [length for _, length, _ in found]
    )
    for grads, to_prefix, to_branch in ((grad_keys, d_prefix_k, d_branch_k), (grad_values, d_prefix_v, d_branch_v)):
        to_prefix[...] = grads[:prefix_rows]
        to_branch[...] = jnp.zeros_like(to_branch)
        for s, b in enumerate(blocks):
            first = prefix_rows + s * block
            piece = grads[first:first + block]
            if s == 0:
                to_branch[b] = piece
            else:
                @pl.when(found[s - 1][2])
                def _():
                    to_branch[b] = piece


def per_device_general(query, d_out, branch_kv, prefix_kv, parents, lengths):
    num_blocks = parents.shape[1]
    slots = max(4, num_blocks // 4) - 1
    block = query.shape[1]
    width = query.shape[2]
    with_features = lax.all_gather(prefix_kv, "smp", axis=1, tiled=True)
    prefix_all = lax.all_gather(with_features, "ctx", axis=0, tiled=True)
    prefix_rows, features = prefix_all.shape
    all_blocks = lax.all_gather(branch_kv[0], "ctx", axis=0)
    group_width = width // HK
    smem = pl.BlockSpec(memory_space=pltpu.SMEM)
    heads = pl.BlockSpec((block, group_width), lambda g: (0, g))
    prefix_k = pl.BlockSpec((prefix_rows, HD), lambda g: (0, g))
    prefix_v = pl.BlockSpec((prefix_rows, HD), lambda g: (0, g + HK))
    branch_k = pl.BlockSpec((num_blocks, block, HD), lambda g: (0, 0, g))
    branch_v = pl.BlockSpec((num_blocks, block, HD), lambda g: (0, 0, g + HK))
    grad_prefix = jax.ShapeDtypeStruct((prefix_rows, features // 2), F32)
    grad_branch = jax.ShapeDtypeStruct((num_blocks, block, features // 2), F32)
    out, d_query, dpk, dpv, dbk, dbv = pl.pallas_call(
        functools.partial(attend_kernel, slots),
        grid=(HK,),
        in_specs=[smem, smem, heads, heads, prefix_k, prefix_v, branch_k, branch_v],
        out_specs=[heads, heads, prefix_k, prefix_k, branch_k, branch_k],
        out_shape=[
            jax.ShapeDtypeStruct((block, width), BF16),
            jax.ShapeDtypeStruct((block, width), BF16),
            grad_prefix, grad_prefix, grad_branch, grad_branch,
        ],
        compiler_params=pltpu.CompilerParams(vmem_limit_bytes=56 * 1024 * 1024),
    )(parents, lengths, query[0], d_out[0], prefix_all, prefix_all, all_blocks, all_blocks)
    spread = jnp.concatenate([dbk, dbv], axis=2).reshape(num_blocks * block, features)
    grad_branch = lax.psum_scatter(spread, "ctx", scatter_dimension=0, tiled=True)
    grad_rows = lax.psum_scatter(jnp.concatenate([dpk, dpv], axis=1), "ctx", scatter_dimension=0, tiled=True)
    grad_prefix_out = lax.psum_scatter(grad_rows, "smp", scatter_dimension=1, tiled=True)
    return out[None], d_query[None], grad_branch.astype(BF16)[None], grad_prefix_out.astype(BF16)


CHUNKS = 4
SLOTS = 3
MESH = pl.DeviceIdType.MESH
VMEM_LIMIT = 56 * 1024 * 1024


def greet(ctx_size, smp_size, me, smp):
    barrier = pltpu.get_barrier_semaphore()
    for d in range(1, ctx_size):
        pl.semaphore_signal(barrier, inc=1, device_id={"ctx": lax.rem(me + d, ctx_size)}, device_id_type=MESH)
    for d in range(1, smp_size):
        pl.semaphore_signal(barrier, inc=1, device_id={"smp": lax.rem(smp + d, smp_size)}, device_id_type=MESH)
    pl.semaphore_wait(barrier, ctx_size + smp_size - 2)


def remote(src, dst, send, recv, to):
    return pltpu.make_async_remote_copy(
        src_ref=src, dst_ref=dst, send_sem=send, recv_sem=recv, device_id=to, device_id_type=MESH
    )


def gather_kernel(
    ctx_size, smp_size, parents, branch, prefix, blocks, prefix_all,
    stage, z_send, y_send, recv, p_send, p_recv, q_send, q_recv,
):
    me, smp = lax.axis_index("ctx"), lax.axis_index("smp")
    side = lax.rem(me, 2)
    beside = me + 1 - 2 * side
    rows = branch.shape[0] // CHUNKS
    p_rows, p_cols = prefix.shape
    greet(ctx_size, smp_size, me, smp)

    def part(c):
        return pl.ds(c * rows, rows)

    def up(src, k, c):
        return remote(src, blocks.at[k, part(c)], z_send.at[k, c], recv.at[k, c], {"ctx": me + 2})

    def across(k, c):
        return remote(branch.at[part(c)], blocks.at[k, part(c)], y_send.at[c], recv.at[k, c], {"ctx": beside})

    def arrived(k, c):
        across(k, c).wait_recv()

    p_own = (pl.ds(pl.multiple_of(me * p_rows, p_rows), p_rows), pl.ds(pl.multiple_of(smp * p_cols, p_cols), p_cols))
    q_own = (slice(None), p_own[1])

    def p_copy(d):
        return remote(prefix, prefix_all.at[p_own], p_send.at[d - 1], p_recv.at[d - 1], {"ctx": lax.rem(me + d, ctx_size)})

    def q_copy(d):
        return remote(
            prefix_all.at[q_own], prefix_all.at[q_own], q_send.at[d - 1], q_recv.at[d - 1],
            {"smp": lax.rem(smp + d, smp_size)},
        )

    for d in range(1, ctx_size):
        p_copy(d).start()
    for device, k in ((0, 0), (1, 1), (2, 2), (4, 3), (5, 3), (6, 3)):
        @pl.when(me == device)
        def _():
            for c in range(CHUNKS):
                across(k, c).start()
                if k < 3:
                    up(branch.at[part(c)], k, c).start()
    prefix_all[p_own] = prefix[...]
    for d in range(1, ctx_size):
        p_copy(d).wait_recv()
    for d in range(1, smp_size):
        q_copy(d).start()

    for device, order in ((0, (1,)), (1, (0,)), (2, (0, 1)), (3, (2, 1, 0))):
        @pl.when(me == device)
        def _():
            for c in range(CHUNKS):
                for k in order:
                    arrived(k, c)
                    up(blocks.at[k, part(c)], k, c).start()

    @pl.when((me == 4) | (me == 5))
    def _():
        first = parents[0, 6]
        second = jnp.where(first >= 0, parents[0, jnp.maximum(first, 0)], -1)
        for c in range(CHUNKS):
            for k in range(4):
                arrived(k, c)
            for k, want in enumerate((first, second)):
                total = jnp.where(want == me, 1.0, 0.0) * branch[part(c)].astype(F32)
                for held, index in ((0, 0), (1, 1), (2, 2), (3, beside)):
                    total += jnp.where(want == index, 1.0, 0.0) * blocks[held, part(c)].astype(F32)
                stage[k, part(c)] = total.astype(BF16)
                up(stage.at[k, part(c)], k, c).start()

    @pl.when(me >= 6)
    def _():
        for c in range(CHUNKS):
            for k in range(2):
                arrived(k, c)

    @pl.when(me == 7)
    def _():
        for c in range(CHUNKS):
            arrived(3, c)

    blocks[4] = branch[...]
    for d in range(1, smp_size):
        q_copy(d).wait_recv()
    for d in range(1, ctx_size):
        p_copy(d).wait_send()
    for d in range(1, smp_size):
        q_copy(d).wait_send()

    @pl.when((me != 3) & (me != 7))
    def _():
        for c in range(CHUNKS):
            across(0, c).wait_send()

    @pl.when(me < 6)
    def _():
        for c in range(CHUNKS):
            for k in range(2):
                up(blocks.at[k, part(c)], k, c).wait_send()

    @pl.when((me == 2) | (me == 3))
    def _():
        for c in range(CHUNKS):
            up(blocks.at[2, part(c)], 2, c).wait_send()


def slot_attend_kernel(
    parents, lengths, query, d_out, prefix_k, prefix_v, block_k, block_v,
    out, d_query, d_prefix, d_slots, d_own,
):
    me = lax.axis_index("ctx")
    group = pl.program_id(0)
    prefix_rows = prefix_k.shape[0]
    block = query.shape[0]
    half = d_own.shape[1] // 2
    found = walk_up(parents, lengths, me, SLOTS)
    held = []
    for s, (index, _, _) in enumerate(found):
        last = 3 if s == 0 else s - 1
        held.append(jnp.where(me < 6, jnp.minimum(index, 3), jnp.where(me == 6, s, last)))
    read = [4] + [jnp.where(found[s][2], held[s], 4) for s in range(SLOTS)]
    keys = jnp.concatenate([prefix_k[...]] + [block_k[b] for b in read], axis=0)
    values = jnp.concatenate([prefix_v[...]] + [block_v[b] for b in read], axis=0)
    out[...], d_query[...], grad_keys, grad_values = attend_group(
        query[...], d_out[...], keys, values, prefix_rows, lengths[0, me], [length for _, length, _ in found]
    )
    for grads, offset in ((grad_keys, 0), (grad_values, half)):
        columns = pl.ds(pl.multiple_of(offset + group * HD, HD), HD)
        d_prefix[:, columns] = grads[:prefix_rows].astype(BF16)
        d_own[:, columns] = grads[prefix_rows:prefix_rows + block]
        d_slots[:, :, columns] = jnp.zeros((4, block, HD), BF16)
        for s in range(SLOTS):
            first = prefix_rows + (s + 1) * block
            piece = grads[first:first + block].astype(BF16)

            @pl.when(found[s][2])
            def _():
                d_slots[held[s], :, columns] = piece


def reduce_kernel(
    ctx_size, smp_size, parents, d_slots, d_own, d_prefix, out, out_prefix,
    below, beside_in, sums, p_in, p_sum, p_low, q_in,
    z_send, z_recv, y_send, y_recv, p_send, p_recv, q_send, q_recv,
):
    me, smp = lax.axis_index("ctx"), lax.axis_index("smp")
    side = lax.rem(me, 2)
    beside = me + 1 - 2 * side
    rows = out.shape[0] // CHUNKS
    p_rows, p_cols = out_prefix.shape
    greet(ctx_size, smp_size, me, smp)

    def part(c):
        return pl.ds(c * rows, rows)

    def down(src, k, c):
        return remote(src, below.at[k, part(c)], z_send.at[k, c], z_recv.at[k, c], {"ctx": me - 2})

    def across(src, c):
        return remote(src, beside_in.at[part(c)], y_send.at[c], y_recv.at[c], {"ctx": beside})

    def from_above(k, c):
        down(sums.at[k, part(c)], k, c).wait_recv()

    def from_beside(c):
        across(sums.at[3, part(c)], c).wait_recv()

    def p_copy(d):
        to = lax.rem(smp + d, smp_size)
        columns = pl.ds(pl.multiple_of(to * p_cols, p_cols), p_cols)
        return remote(d_prefix.at[:, columns], p_in.at[d - 1], p_send.at[d - 1], p_recv.at[d - 1], {"smp": to})

    def q_copy(d):
        to = lax.rem(me + d, ctx_size)
        piece = pl.ds(pl.multiple_of(to * p_rows, p_rows), p_rows)
        return remote(p_low.at[piece], q_in.at[d - 1], q_send.at[d - 1], q_recv.at[d - 1], {"ctx": to})

    def sum_prefix():
        columns = pl.ds(pl.multiple_of(smp * p_cols, p_cols), p_cols)
        for d in range(1, smp_size):
            p_copy(d).wait_recv()
        total = d_prefix[:, columns].astype(F32)
        for d in range(1, smp_size):
            total += p_in[d - 1].astype(F32)
        p_sum[...] = total
        p_low[...] = total.astype(BF16)
        for d in range(1, ctx_size):
            q_copy(d).start()

    def load(ref, k, c):
        return ref[k, part(c)].astype(F32)

    for device in (6, 7):
        @pl.when(me == device)
        def _():
            for c in range(CHUNKS):
                for k in range(2):
                    down(d_slots.at[k, part(c)], k, c).start()
                if device == 7:
                    across(d_slots.at[3, part(c)], c).start()
    for d in range(1, smp_size):
        p_copy(d).start()

    @pl.when((me < 4) | (me >= 6))
    def _():
        sum_prefix()

    @pl.when((me == 4) | (me == 5))
    def _():
        first = parents[0, 6]
        second = jnp.where(first >= 0, parents[0, jnp.maximum(first, 0)], -1)
        for c in range(CHUNKS):
            from_above(0, c)
            from_above(1, c)
            near, far = load(below, 0, c), load(below, 1, c)

            def share(index):
                return jnp.where(first == index, 1.0, 0.0) * near + jnp.where(second == index, 1.0, 0.0) * far

            for k, index in ((0, 0), (1, 1), (2, 2), (3, beside)):
                sums[k, part(c)] = (load(d_slots, k, c) + share(index)).astype(BF16)
                if k < 3:
                    down(sums.at[k, part(c)], k, c).start()
                else:
                    across(sums.at[3, part(c)], c).start()
        sum_prefix()

    for device in (2, 3):
        @pl.when(me == device)
        def _():
            for c in range(CHUNKS):
                for k in range(3):
                    from_above(k, c)
                    if k < 2 or device == 3:
                        sums[k, part(c)] = (load(d_slots, k, c) + load(below, k, c)).astype(BF16)
                    if k < 2:
                        down(sums.at[k, part(c)], k, c).start()
                    elif device == 3:
                        across(sums.at[2, part(c)], c).start()

    for device in (0, 1):
        @pl.when(me == device)
        def _():
            for c in range(CHUNKS):
                for k in range(2):
                    from_above(k, c)
                other = 1 - device
                sums[3, part(c)] = (load(d_slots, other, c) + load(below, other, c)).astype(BF16)
                across(sums.at[3, part(c)], c).start()

    for device, slot in ((0, 0), (1, 1), (2, 2), (6, None), (4, None), (5, None)):
        @pl.when(me == device)
        def _():
            for c in range(CHUNKS):
                from_beside(c)
                total = beside_in[part(c)].astype(F32)
                if slot is not None:
                    total += load(below, slot, c)
                if device in (4, 5):
                    first = parents[0, 6]
                    second = jnp.where(first >= 0, parents[0, jnp.maximum(first, 0)], -1)
                    total += jnp.where(first == me, 1.0, 0.0) * load(below, 0, c)
                    total += jnp.where(second == me, 1.0, 0.0) * load(below, 1, c)
                out[part(c)] = (d_own[part(c)] + total).astype(BF16)

    @pl.when((me == 3) | (me == 7))
    def _():
        out[...] = d_own[...].astype(BF16)

    own_rows = pl.ds(pl.multiple_of(me * p_rows, p_rows), p_rows)
    total = p_sum[own_rows]
    for d in range(1, ctx_size):
        q_copy(d).wait_recv()
        total += q_in[d - 1].astype(F32)
    out_prefix[...] = total.astype(BF16)

    for d in range(1, smp_size):
        p_copy(d).wait_send()
    for d in range(1, ctx_size):
        q_copy(d).wait_send()

    @pl.when((me != 2) & (me != 6))
    def _():
        for c in range(CHUNKS):
            across(sums.at[3, part(c)], c).wait_send()

    @pl.when(me >= 2)
    def _():
        for c in range(CHUNKS):
            for k in range(2):
                down(sums.at[k, part(c)], k, c).wait_send()

    @pl.when((me == 4) | (me == 5))
    def _():
        for c in range(CHUNKS):
            down(sums.at[2, part(c)], 2, c).wait_send()


def per_device(query, d_out, branch_kv, prefix_kv, parents, lengths):
    ctx_size, smp_size = lax.axis_size("ctx"), lax.axis_size("smp")
    if parents.shape[1] != 8 or ctx_size != 8:
        return per_device_general(query, d_out, branch_kv, prefix_kv, parents, lengths)
    block, width = query.shape[1:]
    features = branch_kv.shape[2]
    p_rows, p_cols = prefix_kv.shape
    prefix_rows = p_rows * ctx_size
    group_width = width // HK
    smem = pl.BlockSpec(memory_space=pltpu.SMEM)
    vmem = pl.BlockSpec(memory_space=pltpu.VMEM)
    dma = pltpu.SemaphoreType.DMA
    blocks, prefix_all = pl.pallas_call(
        functools.partial(gather_kernel, ctx_size, smp_size),
        in_specs=[smem, vmem, vmem],
        out_specs=[vmem, vmem],
        out_shape=[
            jax.ShapeDtypeStruct((5, block, features), BF16),
            jax.ShapeDtypeStruct((prefix_rows, features), BF16),
        ],
        scratch_shapes=[
            pltpu.VMEM((2, block, features), BF16),
            dma((3, CHUNKS)), dma((CHUNKS,)), dma((4, CHUNKS)),
            dma((ctx_size - 1,)), dma((ctx_size - 1,)), dma((smp_size - 1,)), dma((smp_size - 1,)),
        ],
        compiler_params=pltpu.CompilerParams(
            collective_id=0, has_side_effects=True, vmem_limit_bytes=VMEM_LIMIT
        ),
        name="gather_blocks",
    )(parents, branch_kv[0], prefix_kv)

    def whole(*shape):
        return pl.BlockSpec(shape, lambda g: (0,) * len(shape))

    heads = pl.BlockSpec((block, group_width), lambda g: (0, g))
    out, d_query, d_prefix, d_slots, d_own = pl.pallas_call(
        slot_attend_kernel,
        grid=(HK,),
        in_specs=[
            smem, smem, heads, heads,
            pl.BlockSpec((prefix_rows, HD), lambda g: (0, g)),
            pl.BlockSpec((prefix_rows, HD), lambda g: (0, g + HK)),
            pl.BlockSpec((5, block, HD), lambda g: (0, 0, g)),
            pl.BlockSpec((5, block, HD), lambda g: (0, 0, g + HK)),
        ],
        out_specs=[heads, heads, whole(prefix_rows, features), whole(4, block, features), whole(block, features)],
        out_shape=[
            jax.ShapeDtypeStruct((block, width), BF16),
            jax.ShapeDtypeStruct((block, width), BF16),
            jax.ShapeDtypeStruct((prefix_rows, features), BF16),
            jax.ShapeDtypeStruct((4, block, features), BF16),
            jax.ShapeDtypeStruct((block, features), F32),
        ],
        compiler_params=pltpu.CompilerParams(vmem_limit_bytes=VMEM_LIMIT),
        name="attend",
    )(parents, lengths, query[0], d_out[0], prefix_all, prefix_all, blocks, blocks)
    d_branch, d_prefix_out = pl.pallas_call(
        functools.partial(reduce_kernel, ctx_size, smp_size),
        in_specs=[smem, vmem, vmem, vmem],
        out_specs=[vmem, vmem],
        out_shape=[
            jax.ShapeDtypeStruct((block, features), BF16),
            jax.ShapeDtypeStruct((p_rows, p_cols), BF16),
        ],
        scratch_shapes=[
            pltpu.VMEM((3, block, features), BF16),
            pltpu.VMEM((block, features), BF16),
            pltpu.VMEM((4, block, features), BF16),
            pltpu.VMEM((smp_size - 1, prefix_rows, p_cols), BF16),
            pltpu.VMEM((prefix_rows, p_cols), F32),
            pltpu.VMEM((prefix_rows, p_cols), BF16),
            pltpu.VMEM((ctx_size - 1, p_rows, p_cols), BF16),
            dma((3, CHUNKS)), dma((3, CHUNKS)), dma((CHUNKS,)), dma((CHUNKS,)),
            dma((smp_size - 1,)), dma((smp_size - 1,)), dma((ctx_size - 1,)), dma((ctx_size - 1,)),
        ],
        compiler_params=pltpu.CompilerParams(
            collective_id=1, has_side_effects=True, vmem_limit_bytes=VMEM_LIMIT
        ),
        name="reduce_grads",
    )(parents, d_slots, d_own, d_prefix)
    return out[None], d_query[None], d_branch[None], d_prefix_out


def solution(mesh):
    return jax.shard_map(
        per_device,
        mesh=mesh,
        in_specs=(
            P("smp", "ctx", None),
            P("smp", "ctx", None),
            P("smp", "ctx", None),
            P("ctx", "smp"),
            P("smp", None),
            P("smp", None),
        ),
        out_specs=(
            P("smp", "ctx", None),
            P("smp", "ctx", None),
            P("smp", "ctx", None),
            P("ctx", "smp"),
        ),
        check_vma=False,
    )
```

```python
import functools
import math

import jax
import jax.numpy as jnp
from jax import lax
from jax.experimental import pallas as pl
from jax.experimental.pallas import tpu as pltpu
from jax.sharding import PartitionSpec as P

HK = 4
HD = 128
F32 = jnp.float32
BF16 = jnp.bfloat16


def walk_up(parents, lengths, start, count):
    found = []
    at = start
    for _ in range(count):
        up = parents[0, jnp.maximum(at, 0)]
        at = jnp.where(at >= 0, up, -1)
        held = jnp.maximum(at, 0)
        found.append((held, jnp.where(at >= 0, lengths[0, held], 0), at >= 0))
    return found


def attend_group(query, d_out, keys, values, prefix_rows, own_length, slot_lengths):
    block = query.shape[0]
    group = query.shape[1] // HD
    scale = HD ** -0.5
    to_exp2 = scale * math.log2(math.e)
    place = lax.broadcasted_iota(jnp.int32, (block, 1), 0)
    grad_live = jnp.where(place < own_length, d_out, jnp.zeros_like(d_out))

    def heads(x):
        return [x[:, h * HD:(h + 1) * HD] for h in range(group)]

    query_rows = jnp.concatenate(heads(query), axis=0)
    grad_rows = jnp.concatenate(heads(grad_live), axis=0)
    grad_cols = jnp.concatenate([h.T for h in heads(grad_live)], axis=1)

    scores = lax.dot_general(keys, query_rows, (((1,), (1,)), ((), ())), preferred_element_type=F32)
    row = lax.broadcasted_iota(jnp.int32, (block, block), 1)
    key = lax.broadcasted_iota(jnp.int32, (block, block), 0)
    own_bias = jnp.where((key < own_length) & (key <= row), 0.0, -jnp.inf)
    own_bias = jnp.concatenate([own_bias] * group, axis=1)
    parts = [scores[:prefix_rows], scores[prefix_rows:prefix_rows + block] + own_bias]
    for s, length in enumerate(slot_lengths):
        first = prefix_rows + (s + 1) * block
        parts.append(scores[first:first + block] + jnp.where(place < length, 0.0, -jnp.inf))
    scores = jnp.concatenate(parts, axis=0)
    top = jnp.max(scores, axis=0, keepdims=True) * to_exp2
    exponent = jnp.exp2(scores * to_exp2 - top)
    probs = exponent * (1.0 / jnp.sum(exponent, axis=0, keepdims=True))
    probs_low = probs.astype(BF16)
    attended = lax.dot_general(values, probs_low, (((0,), (0,)), ((), ())), preferred_element_type=F32)
    live = lax.broadcasted_iota(jnp.int32, (1, block), 1) < own_length
    live = jnp.concatenate([jnp.where(live, 1.0, 0.0)] * group, axis=1)
    attended = (attended * live).astype(BF16)
    delta = jnp.sum(grad_cols.astype(F32) * attended.astype(F32), axis=0, keepdims=True)
    grad_probs = jnp.dot(values, grad_cols, preferred_element_type=F32)
    grad_scores = (probs * (grad_probs - delta)).astype(BF16)
    grad_query = lax.dot_general(keys, grad_scores, (((0,), (0,)), ((), ())), preferred_element_type=F32)
    grad_query = (grad_query * scale).astype(BF16)
    grad_keys = jnp.dot(grad_scores, query_rows, preferred_element_type=F32) * scale
    grad_values = jnp.dot(probs_low, grad_rows, preferred_element_type=F32)
    return (
        jnp.concatenate([h.T for h in heads_across(attended, block)], axis=1),
        jnp.concatenate([h.T for h in heads_across(grad_query, block)], axis=1),
        grad_keys,
        grad_values,
    )


def heads_across(x, block):
    return [x[:, h * block:(h + 1) * block] for h in range(x.shape[1] // block)]


def attend_kernel(
    slots, parents, lengths, query, d_out, prefix_k, prefix_v, branch_k, branch_v,
    out, d_query, d_prefix_k, d_prefix_v, d_branch_k, d_branch_v,
):
    me = lax.axis_index("ctx")
    prefix_rows = prefix_k.shape[0]
    block = query.shape[0]
    found = walk_up(parents, lengths, me, slots)
    blocks = [me] + [index for index, _, _ in found]
    keys = jnp.concatenate([prefix_k[...]] + [branch_k[b] for b in blocks], axis=0)
    values = jnp.concatenate([prefix_v[...]] + [branch_v[b] for b in blocks], axis=0)
    out[...], d_query[...], grad_keys, grad_values = attend_group(
        query[...], d_out[...], keys, values, prefix_rows, lengths[0, me], [length for _, length, _ in found]
    )
    for grads, to_prefix, to_branch in ((grad_keys, d_prefix_k, d_branch_k), (grad_values, d_prefix_v, d_branch_v)):
        to_prefix[...] = grads[:prefix_rows]
        to_branch[...] = jnp.zeros_like(to_branch)
        for s, b in enumerate(blocks):
            first = prefix_rows + s * block
            piece = grads[first:first + block]
            if s == 0:
                to_branch[b] = piece
            else:
                @pl.when(found[s - 1][2])
                def _():
                    to_branch[b] = piece


def per_device_general(query, d_out, branch_kv, prefix_kv, parents, lengths):
    num_blocks = parents.shape[1]
    slots = max(4, num_blocks // 4) - 1
    block = query.shape[1]
    width = query.shape[2]
    with_features = lax.all_gather(prefix_kv, "smp", axis=1, tiled=True)
    prefix_all = lax.all_gather(with_features, "ctx", axis=0, tiled=True)
    prefix_rows, features = prefix_all.shape
    all_blocks = lax.all_gather(branch_kv[0], "ctx", axis=0)
    group_width = width // HK
    smem = pl.BlockSpec(memory_space=pltpu.SMEM)
    heads = pl.BlockSpec((block, group_width), lambda g: (0, g))
    prefix_k = pl.BlockSpec((prefix_rows, HD), lambda g: (0, g))
    prefix_v = pl.BlockSpec((prefix_rows, HD), lambda g: (0, g + HK))
    branch_k = pl.BlockSpec((num_blocks, block, HD), lambda g: (0, 0, g))
    branch_v = pl.BlockSpec((num_blocks, block, HD), lambda g: (0, 0, g + HK))
    grad_prefix = jax.ShapeDtypeStruct((prefix_rows, features // 2), F32)
    grad_branch = jax.ShapeDtypeStruct((num_blocks, block, features // 2), F32)
    out, d_query, dpk, dpv, dbk, dbv = pl.pallas_call(
        functools.partial(attend_kernel, slots),
        grid=(HK,),
        in_specs=[smem, smem, heads, heads, prefix_k, prefix_v, branch_k, branch_v],
        out_specs=[heads, heads, prefix_k, prefix_k, branch_k, branch_k],
        out_shape=[
            jax.ShapeDtypeStruct((block, width), BF16),
            jax.ShapeDtypeStruct((block, width), BF16),
            grad_prefix, grad_prefix, grad_branch, grad_branch,
        ],
        compiler_params=pltpu.CompilerParams(vmem_limit_bytes=56 * 1024 * 1024),
    )(parents, lengths, query[0], d_out[0], prefix_all, prefix_all, all_blocks, all_blocks)
    spread = jnp.concatenate([dbk, dbv], axis=2).reshape(num_blocks * block, features)
    grad_branch = lax.psum_scatter(spread, "ctx", scatter_dimension=0, tiled=True)
    grad_rows = lax.psum_scatter(jnp.concatenate([dpk, dpv], axis=1), "ctx", scatter_dimension=0, tiled=True)
    grad_prefix_out = lax.psum_scatter(grad_rows, "smp", scatter_dimension=1, tiled=True)
    return out[None], d_query[None], grad_branch.astype(BF16)[None], grad_prefix_out.astype(BF16)


SLOTS = 3
MESH = pl.DeviceIdType.MESH
VMEM_LIMIT = 56 * 1024 * 1024


def greet(ctx_size, smp_size, me, smp):
    barrier = pltpu.get_barrier_semaphore()
    for d in range(1, ctx_size):
        pl.semaphore_signal(barrier, inc=1, device_id={"ctx": lax.rem(me + d, ctx_size)}, device_id_type=MESH)
    for d in range(1, smp_size):
        pl.semaphore_signal(barrier, inc=1, device_id={"smp": lax.rem(smp + d, smp_size)}, device_id_type=MESH)
    pl.semaphore_wait(barrier, ctx_size + smp_size - 2)


def remote(src, dst, send, recv, to):
    return pltpu.make_async_remote_copy(
        src_ref=src, dst_ref=dst, send_sem=send, recv_sem=recv, device_id=to, device_id_type=MESH
    )


def tree_kernel(
    ctx_size, smp_size, parents, lengths, query, d_out, branch, prefix,
    out, d_query, d_branch, d_prefix,
    own, held, stage, pre_own, pre, mine, d_own, sums, below, beside_in, d_pre, p_in, p_sum, p_low, q_in,
    up_send, up_recv, over_send, a_send, a_recv, b_send, b_recv,
    down_send, down_recv, back_send, back_recv, p_send, p_recv, q_send, q_recv,
):
    me, smp = lax.axis_index("ctx"), lax.axis_index("smp")
    beside = me + 1 - 2 * lax.rem(me, 2)
    block = branch.shape[0]
    group_width = query.shape[1] // HK
    p_rows = prefix.shape[0]
    prefix_rows = pre.shape[1]
    greet(ctx_size, smp_size, me, smp)

    def up(src, k, c):
        return remote(src, held.at[c, k], up_send.at[k, c], up_recv.at[k, c], {"ctx": me + 2})

    def over(k, c):
        return remote(own.at[c], held.at[c, k], over_send.at[c], up_recv.at[k, c], {"ctx": beside})

    def arrived(k, c):
        over(k, c).wait_recv()

    def down(k, c):
        return remote(sums.at[c, k], below.at[c, k], down_send.at[k, c], down_recv.at[k, c], {"ctx": me - 2})

    def back(k, c):
        return remote(sums.at[c, k], beside_in.at[c], back_send.at[c], back_recv.at[c], {"ctx": beside})

    my_rows = pl.ds(pl.multiple_of(me * p_rows, p_rows), p_rows)
    my_columns = pl.ds(2 * smp, 2)

    def a_copy(d):
        return remote(
            pre_own, pre.at[my_columns, my_rows], a_send.at[d - 1], a_recv.at[d - 1], {"ctx": lax.rem(me + d, ctx_size)}
        )

    def b_copy(d):
        return remote(
            pre.at[my_columns], pre.at[my_columns], b_send.at[d - 1], b_recv.at[d - 1],
            {"smp": lax.rem(smp + d, smp_size)},
        )

    def p_copy(d):
        to = lax.rem(smp + d, smp_size)
        return remote(d_pre.at[pl.ds(2 * to, 2)], p_in.at[d - 1], p_send.at[d - 1], p_recv.at[d - 1], {"smp": to})

    def q_copy(d):
        to = lax.rem(me + d, ctx_size)
        rows = pl.ds(pl.multiple_of(to * p_rows, p_rows), p_rows)
        return remote(p_low.at[:, rows], q_in.at[d - 1], q_send.at[d - 1], q_recv.at[d - 1], {"ctx": to})

    for i in range(2):
        pre_own[i] = prefix[:, i * HD:(i + 1) * HD]
        pre[2 * smp + i, my_rows] = prefix[:, i * HD:(i + 1) * HD]
    for d in range(1, ctx_size):
        a_copy(d).start()
    for c in range(HK):
        own[c, 0] = branch[:, c * HD:(c + 1) * HD]
        own[c, 1] = branch[:, (HK + c) * HD:(HK + c + 1) * HD]
    for device, k in ((0, 0), (1, 1), (2, 2), (4, 3), (5, 3), (6, 3)):
        @pl.when(me == device)
        def _():
            for c in range(HK):
                over(k, c).start()
                if k < 3 and c < 2:
                    up(own.at[c], k, c).start()
    for k, without in ((0, me == 0), (1, me == 1), (2, (me < 3) | (me > 5)), (3, (me < 4) | (me == 6))):
        @pl.when(without)
        def _():
            for c in range(HK):
                held[c, k] = jnp.zeros(held.shape[2:], BF16)
    for d in range(1, ctx_size):
        a_copy(d).wait_recv()
    for d in range(1, smp_size):
        b_copy(d).start()

    first = parents[0, 6]
    second = jnp.where(first >= 0, parents[0, jnp.maximum(first, 0)], -1)
    found = walk_up(parents, lengths, me, SLOTS)
    weight = []
    for s, (index, _, there) in enumerate(found):
        place = jnp.where(me < 6, jnp.minimum(index, 3), jnp.where(me == 6, s, 3 if s == 0 else s - 1))
        weight.append([jnp.where(there & (place == k), 1.0, 0.0) for k in range(4)])

    def forward(c):
        for device, order in ((0, (1,)), (1, (0,)), (2, (0, 1)), (3, (2, 1, 0))):
            @pl.when(me == device)
            def _():
                for k in order:
                    arrived(k, c)
                    up(held.at[c, k], k, c).start()
                if device < 3:
                    @pl.when(c < HK - 2)
                    def _():
                        up(own.at[c + 2], device, c + 2).start()

        @pl.when((me == 4) | (me == 5))
        def _():
            for k in range(4):
                arrived(k, c)
            for k, want in enumerate((first, second)):
                total = jnp.where(want == me, 1.0, 0.0) * own[c].astype(F32)
                for slot, index in ((0, 0), (1, 1), (2, 2), (3, beside)):
                    total += jnp.where(want == index, 1.0, 0.0) * held[c, slot].astype(F32)
                stage[c, k] = total.astype(BF16)
                up(stage.at[c, k], k, c).start()

        @pl.when(me >= 6)
        def _():
            for k in range(2):
                arrived(k, c)

        @pl.when(me == 7)
        def _():
            arrived(3, c)

    def compute(c):
        sides = []
        for i in range(2):
            parts = [pre[HK * i + c], own[c, i]]
            slots = [held[c, k, i].astype(F32) for k in range(4)]
            for w in weight:
                parts.append((w[0] * slots[0] + w[1] * slots[1] + w[2] * slots[2] + w[3] * slots[3]).astype(BF16))
            sides.append(jnp.concatenate(parts, axis=0))
        columns = pl.ds(pl.multiple_of(c * group_width, group_width), group_width)
        out[:, columns], d_query[:, columns], grad_keys, grad_values = attend_group(
            query[:, columns], d_out[:, columns], sides[0], sides[1], prefix_rows, lengths[0, me],
            [length for _, length, _ in found],
        )
        for i, grads in enumerate((grad_keys, grad_values)):
            d_pre[HK * i + c] = grads[:prefix_rows].astype(BF16)
            d_own[c, i] = grads[prefix_rows:prefix_rows + block]
            pieces = [grads[prefix_rows + s * block:prefix_rows + (s + 1) * block] for s in range(1, SLOTS + 1)]
            for k in range(4):
                mine[c, k, i] = weight[0][k] * pieces[0] + weight[1][k] * pieces[1] + weight[2][k] * pieces[2]

        @pl.when(me >= 6)
        def _():
            for k in range(2):
                sums[c, k] = mine[c, k].astype(BF16)
                down(k, c).start()

        @pl.when(me == 7)
        def _():
            sums[c, 3] = mine[c, 3].astype(BF16)
            back(3, c).start()

    def shared(c, index):
        near, far = below[c, 0].astype(F32), below[c, 1].astype(F32)
        return jnp.where(first == index, 1.0, 0.0) * near + jnp.where(second == index, 1.0, 0.0) * far

    def add_down(c):
        @pl.when((me == 4) | (me == 5))
        def _():
            for k in range(2):
                down(k, c).wait_recv()
            for k, index in ((0, 0), (1, 1), (2, 2), (3, beside)):
                sums[c, k] = (mine[c, k] + shared(c, index)).astype(BF16)
                if k < 3:
                    down(k, c).start()
                else:
                    back(3, c).start()

        for device in (2, 3):
            @pl.when(me == device)
            def _():
                for k in range(3):
                    down(k, c).wait_recv()
                    if k < 2 or device == 3:
                        sums[c, k] = (mine[c, k] + below[c, k].astype(F32)).astype(BF16)
                    if k < 2:
                        down(k, c).start()
                    elif device == 3:
                        back(2, c).start()

        for device in (0, 1):
            @pl.when(me == device)
            def _():
                for k in range(2):
                    down(k, c).wait_recv()
                sums[c, 3] = (mine[c, 1 - device] + below[c, 1 - device].astype(F32)).astype(BF16)
                back(3, c).start()

    def sum_prefix():
        for d in range(1, smp_size):
            p_copy(d).wait_recv()
        total = d_pre[my_columns].astype(F32)
        for d in range(1, smp_size):
            total += p_in[d - 1].astype(F32)
        p_sum[...] = total
        p_low[...] = total.astype(BF16)
        for d in range(1, ctx_size):
            q_copy(d).start()

    lag = jnp.where(me >= 6, 0, 1)
    down_lag = jnp.where(me >= 4, 3, 4)
    prefix_step = jnp.where(me >= 6, HK + 1, jnp.where(me >= 4, HK + 3, HK + 2))

    @pl.loop(0, 2 * HK)
    def _(t):
        @pl.when(t < HK)
        def _():
            forward(t)

        @pl.when(t == 0)
        def _():
            for d in range(1, smp_size):
                b_copy(d).wait_recv()

        @pl.when((t >= lag) & (t < HK + lag))
        def _():
            compute(t - lag)

        @pl.when(t == HK)
        def _():
            for d in range(1, smp_size):
                p_copy(d).start()

        @pl.when(t == prefix_step)
        def _():
            sum_prefix()

        @pl.when((t >= down_lag) & (t < HK + down_lag) & (me < 6))
        def _():
            add_down(t - down_lag)

    for device in (0, 1, 2, 4, 5, 6):
        @pl.when(me == device)
        def _():
            for c in range(HK):
                back(3, c).wait_recv()
                total = d_own[c] + beside_in[c].astype(F32)
                if device < 3:
                    total += below[c, device].astype(F32)
                elif device < 6:
                    total += shared(c, me)
                for i in range(2):
                    d_branch[:, (HK * i + c) * HD:(HK * i + c + 1) * HD] = total[i].astype(BF16)

    @pl.when((me == 3) | (me == 7))
    def _():
        for c in range(HK):
            for i in range(2):
                d_branch[:, (HK * i + c) * HD:(HK * i + c + 1) * HD] = d_own[c, i].astype(BF16)

    total = p_sum[:, my_rows]
    for d in range(1, ctx_size):
        q_copy(d).wait_recv()
        total += q_in[d - 1].astype(F32)
    for i in range(2):
        d_prefix[:, i * HD:(i + 1) * HD] = total[i].astype(BF16)

    for d in range(1, ctx_size):
        a_copy(d).wait_send()
        q_copy(d).wait_send()
    for d in range(1, smp_size):
        b_copy(d).wait_send()
        p_copy(d).wait_send()

    def drain(active, copy, slots):
        @pl.when(active)
        def _():
            for c in range(HK):
                for k in slots:
                    copy(k, c).wait_send()

    def climb(k, c):
        return up(held.at[c, k], k, c)

    drain((me != 3) & (me != 7), over, (0,))
    drain(me < 6, climb, (0, 1))
    drain((me == 2) | (me == 3), climb, (2,))
    drain((me != 2) & (me != 6), back, (3,))
    drain(me >= 2, down, (0, 1))
    drain((me == 4) | (me == 5), down, (2,))


def remote(src, dst, send, recv, to):
    return pltpu.make_async_remote_copy(
        src_ref=src, dst_ref=dst, send_sem=send, recv_sem=recv, device_id=to, device_id_type=MESH
    )


def per_device(query, d_out, branch_kv, prefix_kv, parents, lengths):
    ctx_size, smp_size = lax.axis_size("ctx"), lax.axis_size("smp")
    p_rows, p_cols = prefix_kv.shape
    if parents.shape[1] != 8 or ctx_size != 8 or p_cols != 2 * HD:
        return per_device_general(query, d_out, branch_kv, prefix_kv, parents, lengths)
    block, width = query.shape[1:]
    prefix_rows = p_rows * ctx_size
    smem = pl.BlockSpec(memory_space=pltpu.SMEM)
    vmem = pl.BlockSpec(memory_space=pltpu.VMEM)
    dma = pltpu.SemaphoreType.DMA
    pair = (2, block, HD)
    out, d_query, d_branch, d_prefix = pl.pallas_call(
        functools.partial(tree_kernel, ctx_size, smp_size),
        in_specs=[smem, smem, vmem, vmem, vmem, vmem],
        out_specs=[vmem] * 4,
        out_shape=[
            jax.ShapeDtypeStruct((block, width), BF16),
            jax.ShapeDtypeStruct((block, width), BF16),
            jax.ShapeDtypeStruct(branch_kv.shape[1:], BF16),
            jax.ShapeDtypeStruct(prefix_kv.shape, BF16),
        ],
        scratch_shapes=[
            pltpu.VMEM((HK,) + pair, BF16),
            pltpu.VMEM((HK, 4) + pair, BF16),
            pltpu.VMEM((HK, 2) + pair, BF16),
            pltpu.VMEM((2, p_rows, HD), BF16),
            pltpu.VMEM((2 * HK, prefix_rows, HD), BF16),
            pltpu.VMEM((HK, 4) + pair, F32),
            pltpu.VMEM((HK,) + pair, F32),
            pltpu.VMEM((HK, 4) + pair, BF16),
            pltpu.VMEM((HK, 3) + pair, BF16),
            pltpu.VMEM((HK,) + pair, BF16),
            pltpu.VMEM((2 * HK, prefix_rows, HD), BF16),
            pltpu.VMEM((smp_size - 1, 2, prefix_rows, HD), BF16),
            pltpu.VMEM((2, prefix_rows, HD), F32),
            pltpu.VMEM((2, prefix_rows, HD), BF16),
            pltpu.VMEM((ctx_size - 1, 2, p_rows, HD), BF16),
            dma((3, HK)), dma((4, HK)), dma((HK,)),
            dma((ctx_size - 1,)), dma((ctx_size - 1,)), dma((smp_size - 1,)), dma((smp_size - 1,)),
            dma((3, HK)), dma((3, HK)), dma((HK,)), dma((HK,)),
            dma((smp_size - 1,)), dma((smp_size - 1,)), dma((ctx_size - 1,)), dma((ctx_size - 1,)),
        ],
        compiler_params=pltpu.CompilerParams(
            collective_id=0, has_side_effects=True, vmem_limit_bytes=VMEM_LIMIT
        ),
        name="tree_attention",
    )(parents, lengths, query[0], d_out[0], branch_kv[0], prefix_kv)
    return out[None], d_query[None], d_branch[None], d_prefix


def solution(mesh):
    return jax.shard_map(
        per_device,
        mesh=mesh,
        in_specs=(
            P("smp", "ctx", None),
            P("smp", "ctx", None),
            P("smp", "ctx", None),
            P("ctx", "smp"),
            P("smp", None),
            P("smp", None),
        ),
        out_specs=(
            P("smp", "ctx", None),
            P("smp", "ctx", None),
            P("smp", "ctx", None),
            P("ctx", "smp"),
        ),
        check_vma=False,
    )
```

```python
import functools
import math

import jax
import jax.numpy as jnp
from jax import lax
from jax.experimental import pallas as pl
from jax.experimental.pallas import tpu as pltpu
from jax.sharding import PartitionSpec as P

HK = 4
HD = 128
F32 = jnp.float32
BF16 = jnp.bfloat16


def walk_up(parents, lengths, start, count):
    found = []
    at = start
    for _ in range(count):
        up = parents[0, jnp.maximum(at, 0)]
        at = jnp.where(at >= 0, up, -1)
        held = jnp.maximum(at, 0)
        found.append((held, jnp.where(at >= 0, lengths[0, held], 0), at >= 0))
    return found


def attend_group(query, d_out, keys, values, prefix_rows, own_length, slot_lengths):
    block = query.shape[0]
    group = query.shape[1] // HD
    scale = HD ** -0.5
    to_exp2 = scale * math.log2(math.e)
    place = lax.broadcasted_iota(jnp.int32, (block, 1), 0)
    grad_live = jnp.where(place < own_length, d_out, jnp.zeros_like(d_out))

    def heads(x):
        return [x[:, h * HD:(h + 1) * HD] for h in range(group)]

    query_rows = jnp.concatenate(heads(query), axis=0)
    grad_rows = jnp.concatenate(heads(grad_live), axis=0)
    grad_cols = jnp.concatenate([h.T for h in heads(grad_live)], axis=1)

    scores = lax.dot_general(keys, query_rows, (((1,), (1,)), ((), ())), preferred_element_type=F32)
    row = lax.broadcasted_iota(jnp.int32, (block, block), 1)
    key = lax.broadcasted_iota(jnp.int32, (block, block), 0)
    own_bias = jnp.where((key < own_length) & (key <= row), 0.0, -jnp.inf)
    own_bias = jnp.concatenate([own_bias] * group, axis=1)
    parts = [scores[:prefix_rows], scores[prefix_rows:prefix_rows + block] + own_bias]
    for s, length in enumerate(slot_lengths):
        first = prefix_rows + (s + 1) * block
        parts.append(scores[first:first + block] + jnp.where(place < length, 0.0, -jnp.inf))
    scores = jnp.concatenate(parts, axis=0)
    top = jnp.max(scores, axis=0, keepdims=True) * to_exp2
    exponent = jnp.exp2(scores * to_exp2 - top)
    probs = exponent * (1.0 / jnp.sum(exponent, axis=0, keepdims=True))
    probs_low = probs.astype(BF16)
    attended = lax.dot_general(values, probs_low, (((0,), (0,)), ((), ())), preferred_element_type=F32)
    live = lax.broadcasted_iota(jnp.int32, (1, block), 1) < own_length
    live = jnp.concatenate([jnp.where(live, 1.0, 0.0)] * group, axis=1)
    attended = (attended * live).astype(BF16)
    delta = jnp.sum(grad_cols.astype(F32) * attended.astype(F32), axis=0, keepdims=True)
    grad_probs = jnp.dot(values, grad_cols, preferred_element_type=F32)
    grad_scores = (probs * (grad_probs - delta)).astype(BF16)
    grad_query = lax.dot_general(keys, grad_scores, (((0,), (0,)), ((), ())), preferred_element_type=F32)
    grad_query = (grad_query * scale).astype(BF16)
    grad_keys = jnp.dot(grad_scores, query_rows, preferred_element_type=F32) * scale
    grad_values = jnp.dot(probs_low, grad_rows, preferred_element_type=F32)
    return (
        jnp.concatenate([h.T for h in heads_across(attended, block)], axis=1),
        jnp.concatenate([h.T for h in heads_across(grad_query, block)], axis=1),
        grad_keys,
        grad_values,
    )


def heads_across(x, block):
    return [x[:, h * block:(h + 1) * block] for h in range(x.shape[1] // block)]


def attend_kernel(
    slots, parents, lengths, query, d_out, prefix_k, prefix_v, branch_k, branch_v,
    out, d_query, d_prefix_k, d_prefix_v, d_branch_k, d_branch_v,
):
    me = lax.axis_index("ctx")
    prefix_rows = prefix_k.shape[0]
    block = query.shape[0]
    found = walk_up(parents, lengths, me, slots)
    blocks = [me] + [index for index, _, _ in found]
    keys = jnp.concatenate([prefix_k[...]] + [branch_k[b] for b in blocks], axis=0)
    values = jnp.concatenate([prefix_v[...]] + [branch_v[b] for b in blocks], axis=0)
    out[...], d_query[...], grad_keys, grad_values = attend_group(
        query[...], d_out[...], keys, values, prefix_rows, lengths[0, me], [length for _, length, _ in found]
    )
    for grads, to_prefix, to_branch in ((grad_keys, d_prefix_k, d_branch_k), (grad_values, d_prefix_v, d_branch_v)):
        to_prefix[...] = grads[:prefix_rows]
        to_branch[...] = jnp.zeros_like(to_branch)
        for s, b in enumerate(blocks):
            first = prefix_rows + s * block
            piece = grads[first:first + block]
            if s == 0:
                to_branch[b] = piece
            else:
                @pl.when(found[s - 1][2])
                def _():
                    to_branch[b] = piece


def per_device_general(query, d_out, branch_kv, prefix_kv, parents, lengths):
    num_blocks = parents.shape[1]
    slots = max(4, num_blocks // 4) - 1
    block = query.shape[1]
    width = query.shape[2]
    with_features = lax.all_gather(prefix_kv, "smp", axis=1, tiled=True)
    prefix_all = lax.all_gather(with_features, "ctx", axis=0, tiled=True)
    prefix_rows, features = prefix_all.shape
    all_blocks = lax.all_gather(branch_kv[0], "ctx", axis=0)
    group_width = width // HK
    smem = pl.BlockSpec(memory_space=pltpu.SMEM)
    heads = pl.BlockSpec((block, group_width), lambda g: (0, g))
    prefix_k = pl.BlockSpec((prefix_rows, HD), lambda g: (0, g))
    prefix_v = pl.BlockSpec((prefix_rows, HD), lambda g: (0, g + HK))
    branch_k = pl.BlockSpec((num_blocks, block, HD), lambda g: (0, 0, g))
    branch_v = pl.BlockSpec((num_blocks, block, HD), lambda g: (0, 0, g + HK))
    grad_prefix = jax.ShapeDtypeStruct((prefix_rows, features // 2), F32)
    grad_branch = jax.ShapeDtypeStruct((num_blocks, block, features // 2), F32)
    out, d_query, dpk, dpv, dbk, dbv = pl.pallas_call(
        functools.partial(attend_kernel, slots),
        grid=(HK,),
        in_specs=[smem, smem, heads, heads, prefix_k, prefix_v, branch_k, branch_v],
        out_specs=[heads, heads, prefix_k, prefix_k, branch_k, branch_k],
        out_shape=[
            jax.ShapeDtypeStruct((block, width), BF16),
            jax.ShapeDtypeStruct((block, width), BF16),
            grad_prefix, grad_prefix, grad_branch, grad_branch,
        ],
        compiler_params=pltpu.CompilerParams(vmem_limit_bytes=56 * 1024 * 1024),
    )(parents, lengths, query[0], d_out[0], prefix_all, prefix_all, all_blocks, all_blocks)
    spread = jnp.concatenate([dbk, dbv], axis=2).reshape(num_blocks * block, features)
    grad_branch = lax.psum_scatter(spread, "ctx", scatter_dimension=0, tiled=True)
    grad_rows = lax.psum_scatter(jnp.concatenate([dpk, dpv], axis=1), "ctx", scatter_dimension=0, tiled=True)
    grad_prefix_out = lax.psum_scatter(grad_rows, "smp", scatter_dimension=1, tiled=True)
    return out[None], d_query[None], grad_branch.astype(BF16)[None], grad_prefix_out.astype(BF16)


SLOTS = 3
MESH = pl.DeviceIdType.MESH
VMEM_LIMIT = 56 * 1024 * 1024


def greet(ctx_size, smp_size, me, smp):
    barrier = pltpu.get_barrier_semaphore()
    for d in range(1, ctx_size):
        pl.semaphore_signal(barrier, inc=1, device_id={"ctx": lax.rem(me + d, ctx_size)}, device_id_type=MESH)
    for d in range(1, smp_size):
        pl.semaphore_signal(barrier, inc=1, device_id={"smp": lax.rem(smp + d, smp_size)}, device_id_type=MESH)
    pl.semaphore_wait(barrier, ctx_size + smp_size - 2)


def remote(src, dst, send, recv, to):
    return pltpu.make_async_remote_copy(
        src_ref=src, dst_ref=dst, send_sem=send, recv_sem=recv, device_id=to, device_id_type=MESH
    )


def tree_kernel(
    ctx_size, smp_size, parents, lengths, query, d_out, branch, prefix,
    out, d_query, d_branch, d_prefix,
    own, held, stage, pre_own, pre, mine, d_own, other, sums, to_beside, below, other_in, beside_in,
    d_pre, p_in, p_sum, p_low, q_in,
    up_send, up_recv, over_send, over_recv, aside_send, aside_recv, a_send, a_recv, b_send, b_recv,
    down_send, down_recv, cross_send, cross_recv, back_send, back_recv, p_send, p_recv, q_send, q_recv,
):
    me, smp = lax.axis_index("ctx"), lax.axis_index("smp")
    side = lax.rem(me, 2)
    beside = me + 1 - 2 * side
    block = branch.shape[0]
    group_width = query.shape[1] // HK
    p_rows = prefix.shape[0]
    prefix_rows = pre.shape[1]
    greet(ctx_size, smp_size, me, smp)

    def up(src, k, c):
        return remote(src, held.at[c, k, side], up_send.at[k, c], up_recv.at[k, c], {"ctx": me + 2})

    def aside(k, c):
        half = held.at[c, k, side]
        return remote(half, half, aside_send.at[k, c], aside_recv.at[k, c], {"ctx": beside})

    def over(k, c):
        return remote(own.at[c], held.at[c, k], over_send.at[c], over_recv.at[c], {"ctx": beside})

    def over_keys(k, c):
        return remote(own.at[c, 0], held.at[c, k, 0], over_send.at[c], over_recv.at[c], {"ctx": beside})

    def down(k, c):
        return remote(sums.at[c, k], below.at[c, k], down_send.at[k, c], down_recv.at[k, c], {"ctx": me - 2})

    def cross(k, c):
        return remote(other.at[c, k], other_in.at[c, k], cross_send.at[k, c], cross_recv.at[k, c], {"ctx": beside})

    def back(c):
        return remote(to_beside.at[c], beside_in.at[c], back_send.at[c], back_recv.at[c], {"ctx": beside})

    def back_keys(c):
        return remote(to_beside.at[c, 0], beside_in.at[c, 0], back_send.at[c], back_recv.at[c], {"ctx": beside})

    my_rows = pl.ds(pl.multiple_of(me * p_rows, p_rows), p_rows)
    my_columns = pl.ds(2 * smp, 2)

    def a_copy(d):
        return remote(
            pre_own, pre.at[my_columns, my_rows], a_send.at[d - 1], a_recv.at[d - 1], {"ctx": lax.rem(me + d, ctx_size)}
        )

    def b_copy(d):
        return remote(
            pre.at[my_columns], pre.at[my_columns], b_send.at[d - 1], b_recv.at[d - 1],
            {"smp": lax.rem(smp + d, smp_size)},
        )

    def p_copy(d):
        to = lax.rem(smp + d, smp_size)
        return remote(d_pre.at[pl.ds(2 * to, 2)], p_in.at[d - 1], p_send.at[d - 1], p_recv.at[d - 1], {"smp": to})

    def q_copy(d):
        to = lax.rem(me + d, ctx_size)
        rows = pl.ds(pl.multiple_of(to * p_rows, p_rows), p_rows)
        return remote(p_low.at[:, rows], q_in.at[d - 1], q_send.at[d - 1], q_recv.at[d - 1], {"ctx": to})

    for i in range(2):
        pre_own[i] = prefix[:, i * HD:(i + 1) * HD]
        pre[2 * smp + i, my_rows] = prefix[:, i * HD:(i + 1) * HD]
    for d in range(1, ctx_size):
        a_copy(d).start()
    for c in range(HK):
        own[c, 0] = branch[:, c * HD:(c + 1) * HD]
        own[c, 1] = branch[:, (HK + c) * HD:(HK + c + 1) * HD]
    for device, k in ((0, 0), (1, 1), (2, 2), (4, 3), (5, 3), (6, 3)):
        @pl.when(me == device)
        def _():
            for c in range(HK):
                (over_keys if device in (1, 5) else over)(k, c).start()
                if k < 3 and c < 2:
                    up(own.at[c, device % 2], k, c).start()
    for k, without in ((0, me == 0), (1, me < 2), (2, (me < 3) | (me > 5)), (3, (me < 5) | (me == 6))):
        @pl.when(without)
        def _():
            for c in range(HK):
                held[c, k, 1] = jnp.zeros((block, HD), BF16)
    for k, without in ((0, me == 0), (1, me == 1), (2, (me < 3) | (me > 5)), (3, (me < 4) | (me == 6))):
        @pl.when(without)
        def _():
            for c in range(HK):
                held[c, k, 0] = jnp.zeros((block, HD), BF16)
    for d in range(1, ctx_size):
        a_copy(d).wait_recv()
    for d in range(1, smp_size):
        b_copy(d).start()

    first = parents[0, 6]
    second = jnp.where(first >= 0, parents[0, jnp.maximum(first, 0)], -1)
    found = walk_up(parents, lengths, me, SLOTS)
    weight = []
    for s, (index, _, there) in enumerate(found):
        place = jnp.where(me < 6, jnp.minimum(index, 3), jnp.where(me == 6, s, 3 if s == 0 else s - 1))
        weight.append([jnp.where(there & (place == k), 1.0, 0.0) for k in range(4)])

    def forward(c):
        def pass_on(k):
            up(held.at[c, k, side], k, c).wait_recv()
            up(held.at[c, k, side], k, c).start()
            aside(k, c).start()

        def next_own(device):
            @pl.when(c < HK - 2)
            def _():
                up(own.at[c + 2, device % 2], device, c + 2).start()

        @pl.when(me == 0)
        def _():
            over_keys(1, c).wait_recv()
            up(held.at[c, 1, 0], 1, c).start()
            next_own(0)

        @pl.when(me == 1)
        def _():
            over(0, c).wait_recv()
            up(held.at[c, 0, 1], 0, c).start()
            next_own(1)

        @pl.when(me == 2)
        def _():
            pass_on(0)
            pass_on(1)
            next_own(2)

        @pl.when(me == 3)
        def _():
            over(2, c).wait_recv()
            up(held.at[c, 2, 1], 2, c).start()
            pass_on(1)
            pass_on(0)

        @pl.when((me == 4) | (me == 5))
        def _():
            for k in range(3):
                up(held.at[c, k, side], k, c).wait_recv()
                aside(k, c).start()

        @pl.when(me == 4)
        def _():
            over_keys(3, c).wait_recv()

        @pl.when(me == 5)
        def _():
            over(3, c).wait_recv()

        @pl.when((me == 4) | (me == 5))
        def _():
            for k, want in enumerate((first, second)):
                total = jnp.where(want == me, 1.0, 0.0) * own[c, side].astype(F32)
                for slot, index in ((0, 0), (1, 1), (2, 2), (3, beside)):
                    total += jnp.where(want == index, 1.0, 0.0) * held[c, slot, side].astype(F32)
                stage[c, k] = total.astype(BF16)
                up(stage.at[c, k], k, c).start()

        @pl.when(me >= 6)
        def _():
            for k in range(2):
                up(held.at[c, k, side], k, c).wait_recv()
                aside(k, c).start()

        @pl.when(me == 7)
        def _():
            over(3, c).wait_recv()

    def settle(c):
        @pl.when(me >= 2)
        def _():
            for k in range(2):
                aside(k, c).wait_recv()

        @pl.when((me == 4) | (me == 5))
        def _():
            aside(2, c).wait_recv()

    def compute(c):
        sides = []
        for i in range(2):
            parts = [pre[HK * i + c], own[c, i]]
            slots = [held[c, k, i].astype(F32) for k in range(4)]
            for w in weight:
                parts.append((w[0] * slots[0] + w[1] * slots[1] + w[2] * slots[2] + w[3] * slots[3]).astype(BF16))
            sides.append(jnp.concatenate(parts, axis=0))
        columns = pl.ds(pl.multiple_of(c * group_width, group_width), group_width)
        out[:, columns], d_query[:, columns], grad_keys, grad_values = attend_group(
            query[:, columns], d_out[:, columns], sides[0], sides[1], prefix_rows, lengths[0, me],
            [length for _, length, _ in found],
        )
        for i, grads in enumerate((grad_keys, grad_values)):
            d_pre[HK * i + c] = grads[:prefix_rows].astype(BF16)
            d_own[c, i] = grads[prefix_rows:prefix_rows + block]
            pieces = [grads[prefix_rows + s * block:prefix_rows + (s + 1) * block] for s in range(1, SLOTS + 1)]
            for k in range(4):
                mine[c, k, i] = weight[0][k] * pieces[0] + weight[1][k] * pieces[1] + weight[2][k] * pieces[2]

        @pl.when(me >= 2)
        def _():
            for k in range(2):
                other[c, k] = mine[c, k, 1 - side].astype(BF16)
                cross(k, c).start()

        @pl.when((me == 4) | (me == 5))
        def _():
            other[c, 2] = mine[c, 2, 1 - side].astype(BF16)
            cross(2, c).start()

        @pl.when(me == 7)
        def _():
            to_beside[c] = mine[c, 3].astype(BF16)
            back(c).start()

    def shared(c, index):
        near, far = below[c, 0].astype(F32), below[c, 1].astype(F32)
        return jnp.where(first == index, 1.0, 0.0) * near + jnp.where(second == index, 1.0, 0.0) * far

    def add_down(c):
        def send_sum(k, more):
            cross(k, c).wait_recv()
            total = mine[c, k, side] + other_in[c, k].astype(F32)
            if more is not None:
                total += more
            sums[c, k] = total.astype(BF16)
            down(k, c).start()

        @pl.when(me >= 6)
        def _():
            for k in range(2):
                send_sum(k, None)

        @pl.when((me == 4) | (me == 5))
        def _():
            for k in range(2):
                down(k, c).wait_recv()
            for k in range(3):
                send_sum(k, shared(c, k))

        @pl.when(me == 4)
        def _():
            to_beside[c, 0] = (mine[c, 3, 0] + shared(c, 5)).astype(BF16)
            back_keys(c).start()

        @pl.when(me == 5)
        def _():
            to_beside[c, 0] = mine[c, 3, 0].astype(BF16)
            to_beside[c, 1] = (mine[c, 3, 1] + shared(c, 4)).astype(BF16)
            back(c).start()

        @pl.when((me == 2) | (me == 3))
        def _():
            for k in range(2):
                down(k, c).wait_recv()
                send_sum(k, below[c, k].astype(F32))
            down(2, c).wait_recv()

        @pl.when(me == 3)
        def _():
            to_beside[c, 0] = mine[c, 2, 0].astype(BF16)
            to_beside[c, 1] = (mine[c, 2, 1] + below[c, 2].astype(F32)).astype(BF16)
            back(c).start()

        @pl.when(me < 2)
        def _():
            for k in range(2):
                down(k, c).wait_recv()

        @pl.when(me == 0)
        def _():
            to_beside[c, 0] = (mine[c, 1, 0] + below[c, 1].astype(F32)).astype(BF16)
            back_keys(c).start()

        @pl.when(me == 1)
        def _():
            to_beside[c, 0] = mine[c, 0, 0].astype(BF16)
            to_beside[c, 1] = (mine[c, 0, 1] + below[c, 0].astype(F32)).astype(BF16)
            back(c).start()

    def sum_prefix():
        for d in range(1, smp_size):
            p_copy(d).wait_recv()
        total = d_pre[my_columns].astype(F32)
        for d in range(1, smp_size):
            total += p_in[d - 1].astype(F32)
        p_sum[...] = total
        p_low[...] = total.astype(BF16)
        for d in range(1, ctx_size):
            q_copy(d).start()

    down_lag = jnp.where(me >= 6, 2, jnp.where(me >= 4, 3, 4))
    prefix_step = jnp.where(me >= 6, HK + 2, jnp.where(me >= 4, HK + 3, HK + 2))

    @pl.loop(0, 2 * HK)
    def _(t):
        @pl.when(t < HK)
        def _():
            forward(t)

        @pl.when(t == 0)
        def _():
            for d in range(1, smp_size):
                b_copy(d).wait_recv()

        @pl.when((t >= 1) & (t < HK + 1))
        def _():
            settle(t - 1)
            compute(t - 1)

        @pl.when(t == HK)
        def _():
            for d in range(1, smp_size):
                p_copy(d).start()

        @pl.when(t == prefix_step)
        def _():
            sum_prefix()

        @pl.when((t >= down_lag) & (t < HK + down_lag))
        def _():
            add_down(t - down_lag)

    for device in (0, 1, 2, 4, 5, 6):
        @pl.when(me == device)
        def _():
            for c in range(HK):
                if device in (1, 5):
                    back_keys(c).wait_recv()
                else:
                    back(c).wait_recv()
                for i in range(2):
                    total = d_own[c, i]
                    if i == 0 or device not in (1, 5):
                        total += beside_in[c, i].astype(F32)
                    if i == device % 2 and device < 3:
                        total += below[c, device].astype(F32)
                    elif i == device % 2 and device < 6:
                        total += shared(c, device)
                    d_branch[:, (HK * i + c) * HD:(HK * i + c + 1) * HD] = total.astype(BF16)

    @pl.when((me == 3) | (me == 7))
    def _():
        for c in range(HK):
            for i in range(2):
                d_branch[:, (HK * i + c) * HD:(HK * i + c + 1) * HD] = d_own[c, i].astype(BF16)

    total = p_sum[:, my_rows]
    for d in range(1, ctx_size):
        q_copy(d).wait_recv()
        total += q_in[d - 1].astype(F32)
    for i in range(2):
        d_prefix[:, i * HD:(i + 1) * HD] = total[i].astype(BF16)

    for d in range(1, ctx_size):
        a_copy(d).wait_send()
        q_copy(d).wait_send()
    for d in range(1, smp_size):
        b_copy(d).wait_send()
        p_copy(d).wait_send()

    def drain(active, copies):
        @pl.when(active)
        def _():
            for c in range(HK):
                for copy in copies:
                    copy(c).wait_send()

    def on(copy, k):
        return lambda c: copy(k, c)

    def climb(k):
        return lambda c: up(stage.at[c, 0], k, c)

    even = (me == 0) | (me == 2) | (me == 4) | (me == 6)
    drain(even, (on(over, 0),))
    drain((me == 1) | (me == 5), (on(over_keys, 1),))
    drain(me < 6, (climb(0), climb(1)))
    drain((me == 2) | (me == 3), (climb(2),))
    drain(me >= 2, (on(aside, 0), on(aside, 1), on(cross, 0), on(cross, 1), on(down, 0), on(down, 1)))
    drain((me == 4) | (me == 5), (on(aside, 2), on(cross, 2), on(down, 2)))
    drain(side == 1, (back,))
    drain((me == 0) | (me == 4), (back_keys,))


def hand_over_kernel(a, b, c, d, a_out, b_out, c_out, d_out, sem):
    copies = [
        pltpu.make_async_copy(src, dst, sem.at[i])
        for i, (src, dst) in enumerate(((a, a_out), (b, b_out), (c, c_out), (d, d_out)))
    ]
    for copy in copies:
        copy.start()
    for copy in copies:
        copy.wait()


def per_device(query, d_out, branch_kv, prefix_kv, parents, lengths):
    ctx_size, smp_size = lax.axis_size("ctx"), lax.axis_size("smp")
    p_rows, p_cols = prefix_kv.shape
    if parents.shape[1] != 8 or ctx_size != 8 or p_cols != 2 * HD:
        return per_device_general(query, d_out, branch_kv, prefix_kv, parents, lengths)
    block, width = query.shape[1:]
    prefix_rows = p_rows * ctx_size
    smem = pl.BlockSpec(memory_space=pltpu.SMEM)
    vmem = pl.BlockSpec(memory_space=pltpu.VMEM)
    dma = pltpu.SemaphoreType.DMA
    half = (block, HD)
    pair = (2,) + half
    results = pl.pallas_call(
        functools.partial(tree_kernel, ctx_size, smp_size),
        in_specs=[smem, smem, vmem, vmem, vmem, vmem],
        out_specs=[vmem] * 4,
        out_shape=[
            jax.ShapeDtypeStruct((block, width), BF16),
            jax.ShapeDtypeStruct((block, width), BF16),
            jax.ShapeDtypeStruct(branch_kv.shape[1:], BF16),
            jax.ShapeDtypeStruct(prefix_kv.shape, BF16),
        ],
        scratch_shapes=[
            pltpu.VMEM((HK,) + pair, BF16),
            pltpu.VMEM((HK, 4) + pair, BF16),
            pltpu.VMEM((HK, 2) + half, BF16),
            pltpu.VMEM((2, p_rows, HD), BF16),
            pltpu.VMEM((2 * HK, prefix_rows, HD), BF16),
            pltpu.VMEM((HK, 4) + pair, F32),
            pltpu.VMEM((HK,) + pair, F32),
            pltpu.VMEM((HK, 3) + half, BF16),
            pltpu.VMEM((HK, 3) + half, BF16),
            pltpu.VMEM((HK,) + pair, BF16),
            pltpu.VMEM((HK, 3) + half, BF16),
            pltpu.VMEM((HK, 3) + half, BF16),
            pltpu.VMEM((HK,) + pair, BF16),
            pltpu.VMEM((2 * HK, prefix_rows, HD), BF16),
            pltpu.VMEM((smp_size - 1, 2, prefix_rows, HD), BF16),
            pltpu.VMEM((2, prefix_rows, HD), F32),
            pltpu.VMEM((2, prefix_rows, HD), BF16),
            pltpu.VMEM((ctx_size - 1, 2, p_rows, HD), BF16),
            dma((3, HK)), dma((3, HK)), dma((HK,)), dma((HK,)), dma((3, HK)), dma((3, HK)),
            dma((ctx_size - 1,)), dma((ctx_size - 1,)), dma((smp_size - 1,)), dma((smp_size - 1,)),
            dma((3, HK)), dma((3, HK)), dma((3, HK)), dma((3, HK)), dma((HK,)), dma((HK,)),
            dma((smp_size - 1,)), dma((smp_size - 1,)), dma((ctx_size - 1,)), dma((ctx_size - 1,)),
        ],
        compiler_params=pltpu.CompilerParams(
            collective_id=0, has_side_effects=True, vmem_limit_bytes=VMEM_LIMIT
        ),
        name="tree_attention",
    )(parents, lengths, query[0], d_out[0], branch_kv[0], prefix_kv)
    anywhere = pl.BlockSpec(memory_space=pl.ANY)
    out, d_query, d_branch, d_prefix = pl.pallas_call(
        hand_over_kernel,
        in_specs=[anywhere] * 4,
        out_specs=[anywhere] * 4,
        out_shape=[jax.ShapeDtypeStruct(x.shape, x.dtype) for x in results],
        scratch_shapes=[dma((4,))],
        name="hand_over",
    )(*results)
    return out[None], d_query[None], d_branch[None], d_prefix


def solution(mesh):
    return jax.shard_map(
        per_device,
        mesh=mesh,
        in_specs=(
            P("smp", "ctx", None),
            P("smp", "ctx", None),
            P("smp", "ctx", None),
            P("ctx", "smp"),
            P("smp", None),
            P("smp", None),
        ),
        out_specs=(
            P("smp", "ctx", None),
            P("smp", "ctx", None),
            P("smp", "ctx", None),
            P("ctx", "smp"),
        ),
        check_vma=False,
    )
```

```python
import functools
import math

import jax
import jax.numpy as jnp
from jax import lax
from jax.experimental import pallas as pl
from jax.experimental.pallas import tpu as pltpu
from jax.sharding import PartitionSpec as P

HK = 4
HD = 128
F32 = jnp.float32
BF16 = jnp.bfloat16


def walk_up(parents, lengths, start, count):
    found = []
    at = start
    for _ in range(count):
        up = parents[0, jnp.maximum(at, 0)]
        at = jnp.where(at >= 0, up, -1)
        held = jnp.maximum(at, 0)
        found.append((held, jnp.where(at >= 0, lengths[0, held], 0), at >= 0))
    return found


def attend_group(query, d_out, keys, values, prefix_rows, own_length, slot_lengths):
    block = query.shape[0]
    group = query.shape[1] // HD
    scale = HD ** -0.5
    to_exp2 = scale * math.log2(math.e)
    place = lax.broadcasted_iota(jnp.int32, (block, 1), 0)
    grad_live = jnp.where(place < own_length, d_out, jnp.zeros_like(d_out))

    def heads(x):
        return [x[:, h * HD:(h + 1) * HD] for h in range(group)]

    query_rows = jnp.concatenate(heads(query), axis=0)
    grad_rows = jnp.concatenate(heads(grad_live), axis=0)
    grad_cols = jnp.concatenate([h.T for h in heads(grad_live)], axis=1)

    scores = lax.dot_general(keys, query_rows, (((1,), (1,)), ((), ())), preferred_element_type=F32)
    row = lax.broadcasted_iota(jnp.int32, (block, block), 1)
    key = lax.broadcasted_iota(jnp.int32, (block, block), 0)
    own_bias = jnp.where((key < own_length) & (key <= row), 0.0, -jnp.inf)
    own_bias = jnp.concatenate([own_bias] * group, axis=1)
    parts = [scores[:prefix_rows], scores[prefix_rows:prefix_rows + block] + own_bias]
    for s, length in enumerate(slot_lengths):
        first = prefix_rows + (s + 1) * block
        parts.append(scores[first:first + block] + jnp.where(place < length, 0.0, -jnp.inf))
    scores = jnp.concatenate(parts, axis=0)
    top = jnp.max(scores, axis=0, keepdims=True) * to_exp2
    exponent = jnp.exp2(scores * to_exp2 - top)
    probs = exponent * (1.0 / jnp.sum(exponent, axis=0, keepdims=True))
    probs_low = probs.astype(BF16)
    attended = lax.dot_general(values, probs_low, (((0,), (0,)), ((), ())), preferred_element_type=F32)
    live = lax.broadcasted_iota(jnp.int32, (1, block), 1) < own_length
    live = jnp.concatenate([jnp.where(live, 1.0, 0.0)] * group, axis=1)
    attended = (attended * live).astype(BF16)
    delta = jnp.sum(grad_cols.astype(F32) * attended.astype(F32), axis=0, keepdims=True)
    grad_probs = jnp.dot(values, grad_cols, preferred_element_type=F32)
    grad_scores = (probs * (grad_probs - delta)).astype(BF16)
    grad_query = lax.dot_general(keys, grad_scores, (((0,), (0,)), ((), ())), preferred_element_type=F32)
    grad_query = (grad_query * scale).astype(BF16)
    grad_keys = jnp.dot(grad_scores, query_rows, preferred_element_type=F32) * scale
    grad_values = jnp.dot(probs_low, grad_rows, preferred_element_type=F32)
    return (
        jnp.concatenate([h.T for h in heads_across(attended, block)], axis=1),
        jnp.concatenate([h.T for h in heads_across(grad_query, block)], axis=1),
        grad_keys,
        grad_values,
    )


def heads_across(x, block):
    return [x[:, h * block:(h + 1) * block] for h in range(x.shape[1] // block)]


def attend_kernel(
    slots, parents, lengths, query, d_out, prefix_k, prefix_v, branch_k, branch_v,
    out, d_query, d_prefix_k, d_prefix_v, d_branch_k, d_branch_v,
):
    me = lax.axis_index("ctx")
    prefix_rows = prefix_k.shape[0]
    block = query.shape[0]
    found = walk_up(parents, lengths, me, slots)
    blocks = [me] + [index for index, _, _ in found]
    keys = jnp.concatenate([prefix_k[...]] + [branch_k[b] for b in blocks], axis=0)
    values = jnp.concatenate([prefix_v[...]] + [branch_v[b] for b in blocks], axis=0)
    out[...], d_query[...], grad_keys, grad_values = attend_group(
        query[...], d_out[...], keys, values, prefix_rows, lengths[0, me], [length for _, length, _ in found]
    )
    for grads, to_prefix, to_branch in ((grad_keys, d_prefix_k, d_branch_k), (grad_values, d_prefix_v, d_branch_v)):
        to_prefix[...] = grads[:prefix_rows]
        to_branch[...] = jnp.zeros_like(to_branch)
        for s, b in enumerate(blocks):
            first = prefix_rows + s * block
            piece = grads[first:first + block]
            if s == 0:
                to_branch[b] = piece
            else:
                @pl.when(found[s - 1][2])
                def _():
                    to_branch[b] = piece


def per_device_general(query, d_out, branch_kv, prefix_kv, parents, lengths):
    num_blocks = parents.shape[1]
    slots = max(4, num_blocks // 4) - 1
    block = query.shape[1]
    width = query.shape[2]
    with_features = lax.all_gather(prefix_kv, "smp", axis=1, tiled=True)
    prefix_all = lax.all_gather(with_features, "ctx", axis=0, tiled=True)
    prefix_rows, features = prefix_all.shape
    all_blocks = lax.all_gather(branch_kv[0], "ctx", axis=0)
    group_width = width // HK
    smem = pl.BlockSpec(memory_space=pltpu.SMEM)
    heads = pl.BlockSpec((block, group_width), lambda g: (0, g))
    prefix_k = pl.BlockSpec((prefix_rows, HD), lambda g: (0, g))
    prefix_v = pl.BlockSpec((prefix_rows, HD), lambda g: (0, g + HK))
    branch_k = pl.BlockSpec((num_blocks, block, HD), lambda g: (0, 0, g))
    branch_v = pl.BlockSpec((num_blocks, block, HD), lambda g: (0, 0, g + HK))
    grad_prefix = jax.ShapeDtypeStruct((prefix_rows, features // 2), F32)
    grad_branch = jax.ShapeDtypeStruct((num_blocks, block, features // 2), F32)
    out, d_query, dpk, dpv, dbk, dbv = pl.pallas_call(
        functools.partial(attend_kernel, slots),
        grid=(HK,),
        in_specs=[smem, smem, heads, heads, prefix_k, prefix_v, branch_k, branch_v],
        out_specs=[heads, heads, prefix_k, prefix_k, branch_k, branch_k],
        out_shape=[
            jax.ShapeDtypeStruct((block, width), BF16),
            jax.ShapeDtypeStruct((block, width), BF16),
            grad_prefix, grad_prefix, grad_branch, grad_branch,
        ],
        compiler_params=pltpu.CompilerParams(vmem_limit_bytes=56 * 1024 * 1024),
    )(parents, lengths, query[0], d_out[0], prefix_all, prefix_all, all_blocks, all_blocks)
    spread = jnp.concatenate([dbk, dbv], axis=2).reshape(num_blocks * block, features)
    grad_branch = lax.psum_scatter(spread, "ctx", scatter_dimension=0, tiled=True)
    grad_rows = lax.psum_scatter(jnp.concatenate([dpk, dpv], axis=1), "ctx", scatter_dimension=0, tiled=True)
    grad_prefix_out = lax.psum_scatter(grad_rows, "smp", scatter_dimension=1, tiled=True)
    return out[None], d_query[None], grad_branch.astype(BF16)[None], grad_prefix_out.astype(BF16)


SLOTS = 3
MESH = pl.DeviceIdType.MESH
VMEM_LIMIT = 56 * 1024 * 1024


def greet(ctx_size, smp_size, me, smp):
    barrier = pltpu.get_barrier_semaphore()
    for d in range(1, ctx_size):
        pl.semaphore_signal(barrier, inc=1, device_id={"ctx": lax.rem(me + d, ctx_size)}, device_id_type=MESH)
    for d in range(1, smp_size):
        pl.semaphore_signal(barrier, inc=1, device_id={"smp": lax.rem(smp + d, smp_size)}, device_id_type=MESH)
    pl.semaphore_wait(barrier, ctx_size + smp_size - 2)


def remote(src, dst, send, recv, to):
    return pltpu.make_async_remote_copy(
        src_ref=src, dst_ref=dst, send_sem=send, recv_sem=recv, device_id=to, device_id_type=MESH
    )


HEAD_ORDER = (0, 2, 1, 3)


def block_columns(i):
    return slice(i * HD, (i + 1) * HD)


def tree_kernel(
    ctx_size, smp_size, parents, lengths, query_far, d_out_far, branch, prefix,
    out_far, d_query_far, d_branch, d_prefix,
    query, d_out, out, d_query, load_sem, store_sem,
    own, held, stage, pre_own, pre, mine, d_own, other, sums, to_beside, below, other_in, beside_in,
    d_pre, p_in, p_sum, p_low, q_in,
    up_send, up_recv, over_send, over_recv, aside_send, aside_recv, a_send, a_recv, b_send, b_recv,
    down_send, down_recv, cross_send, cross_recv, back_send, back_recv, p_send, p_recv, q_send, q_recv,
):
    me, smp = lax.axis_index("ctx"), lax.axis_index("smp")
    side = lax.rem(me, 2)
    beside = me + 1 - 2 * side
    block = branch.shape[0]
    group_width = query.shape[1] // HK
    p_rows = prefix.shape[0]
    prefix_rows = pre.shape[1]
    loads = [
        pltpu.make_async_copy(query_far, query, load_sem.at[0]), pltpu.make_async_copy(d_out_far, d_out, load_sem.at[1])
    ]
    for load in loads:
        load.start()
    greet(ctx_size, smp_size, me, smp)

    def up(src, k, c):
        return remote(src, held.at[c, k, side], up_send.at[k, c], up_recv.at[k, c], {"ctx": me + 2})

    def aside(k, c):
        half = held.at[c, k, side]
        return remote(half, half, aside_send.at[k, c], aside_recv.at[k, c], {"ctx": beside})

    def over(k, c):
        return remote(own.at[c], held.at[c, k], over_send.at[c], over_recv.at[c], {"ctx": beside})

    def over_keys(k, c):
        return remote(own.at[c, 0], held.at[c, k, 0], over_send.at[c], over_recv.at[c], {"ctx": beside})

    def down(k, c):
        return remote(sums.at[c, k], below.at[c, k], down_send.at[k, c], down_recv.at[k, c], {"ctx": me - 2})

    def cross(k, c):
        return remote(other.at[c, k], other_in.at[c, k], cross_send.at[k, c], cross_recv.at[k, c], {"ctx": beside})

    def back(c):
        return remote(to_beside.at[c], beside_in.at[c], back_send.at[c], back_recv.at[c], {"ctx": beside})

    def back_keys(c):
        return remote(to_beside.at[c, 0], beside_in.at[c, 0], back_send.at[c], back_recv.at[c], {"ctx": beside})

    my_rows = pl.ds(pl.multiple_of(me * p_rows, p_rows), p_rows)
    my_columns = pl.ds(2 * smp, 2)

    def a_copy(d):
        return remote(
            pre_own, pre.at[my_columns, my_rows], a_send.at[d - 1], a_recv.at[d - 1], {"ctx": lax.rem(me + d, ctx_size)}
        )

    def b_copy(d, i):
        columns = pre.at[2 * smp + i]
        return remote(columns, columns, b_send.at[d - 1, i], b_recv.at[d - 1, i], {"smp": lax.rem(smp + d, smp_size)})

    def p_copy(to, d, i):
        return remote(
            d_pre.at[2 * to + i], p_in.at[d - 1, i], p_send.at[d - 1, i], p_recv.at[d - 1, i], {"smp": to}
        )

    def p_after(d, i):
        return p_copy(lax.rem(smp + d, smp_size), d, i)

    def head_columns(c):
        head = 2 * lax.rem(c, 2) + lax.div(c, 2)
        return pl.ds(pl.multiple_of(head * group_width, group_width), group_width)

    def stores(c):
        columns = head_columns(c)
        return [
            pltpu.make_async_copy(src.at[:, columns], dst.at[:, columns], store_sem.at[i, c])
            for i, (src, dst) in enumerate(((out, out_far), (d_query, d_query_far)))
        ]

    def q_copy(d):
        to = lax.rem(me + d, ctx_size)
        rows = pl.ds(pl.multiple_of(to * p_rows, p_rows), p_rows)
        return remote(p_low.at[:, rows], q_in.at[d - 1], q_send.at[d - 1], q_recv.at[d - 1], {"ctx": to})

    for i in range(2):
        pre_own[i] = prefix[:, i * HD:(i + 1) * HD]
        pre[2 * smp + i, my_rows] = prefix[:, i * HD:(i + 1) * HD]
    for d in range(1, ctx_size):
        a_copy(d).start()
    for c in range(HK):
        for i in range(2):
            own[c, i] = branch[:, block_columns(HK * i + HEAD_ORDER[c])]
    for device, k in ((0, 0), (1, 1), (2, 2), (4, 3), (5, 3), (6, 3)):
        @pl.when(me == device)
        def _():
            for c in range(2):
                (over_keys if device in (1, 5) else over)(k, c).start()
                if k < 3:
                    up(own.at[c, device % 2], k, c).start()
    for k, without in ((0, me == 0), (1, me < 2), (2, (me < 3) | (me > 5)), (3, (me < 5) | (me == 6))):
        @pl.when(without)
        def _():
            for c in range(HK):
                held[c, k, 1] = jnp.zeros((block, HD), BF16)
    for k, without in ((0, me == 0), (1, me == 1), (2, (me < 3) | (me > 5)), (3, (me < 4) | (me == 6))):
        @pl.when(without)
        def _():
            for c in range(HK):
                held[c, k, 0] = jnp.zeros((block, HD), BF16)
    for d in range(1, ctx_size):
        a_copy(d).wait_recv()
    for i in range(2):
        for d in range(1, smp_size):
            b_copy(d, i).start()

    first = parents[0, 6]
    second = jnp.where(first >= 0, parents[0, jnp.maximum(first, 0)], -1)
    found = walk_up(parents, lengths, me, SLOTS)
    weight = []
    for s, (index, _, there) in enumerate(found):
        place = jnp.where(me < 6, jnp.minimum(index, 3), jnp.where(me == 6, s, 3 if s == 0 else s - 1))
        weight.append([jnp.where(there & (place == k), 1.0, 0.0) for k in range(4)])

    def forward(c):
        def pass_on(k):
            up(held.at[c, k, side], k, c).wait_recv()
            up(held.at[c, k, side], k, c).start()
            aside(k, c).start()

        @pl.when(me == 0)
        def _():
            over_keys(1, c).wait_recv()
            up(held.at[c, 1, 0], 1, c).start()

        @pl.when(me == 1)
        def _():
            over(0, c).wait_recv()
            up(held.at[c, 0, 1], 0, c).start()

        @pl.when(me == 2)
        def _():
            pass_on(0)
            pass_on(1)

        @pl.when(me == 3)
        def _():
            over(2, c).wait_recv()
            up(held.at[c, 2, 1], 2, c).start()
            pass_on(1)
            pass_on(0)

        @pl.when((me == 4) | (me == 5))
        def _():
            for k in range(3):
                up(held.at[c, k, side], k, c).wait_recv()
                aside(k, c).start()

        @pl.when(me == 4)
        def _():
            over_keys(3, c).wait_recv()

        @pl.when(me == 5)
        def _():
            over(3, c).wait_recv()

        @pl.when((me == 4) | (me == 5))
        def _():
            for k, want in enumerate((first, second)):
                total = jnp.where(want == me, 1.0, 0.0) * own[c, side].astype(F32)
                for slot, index in ((0, 0), (1, 1), (2, 2), (3, beside)):
                    total += jnp.where(want == index, 1.0, 0.0) * held[c, slot, side].astype(F32)
                stage[c, k] = total.astype(BF16)
                up(stage.at[c, k], k, c).start()

        @pl.when(me >= 6)
        def _():
            for k in range(2):
                up(held.at[c, k, side], k, c).wait_recv()
                aside(k, c).start()

        @pl.when(me == 7)
        def _():
            over(3, c).wait_recv()

        for device, k in ((0, 0), (1, 1), (2, 2), (4, 3), (5, 3), (6, 3)):
            @pl.when((me == device) & (c < HK - 2))
            def _():
                (over_keys if device in (1, 5) else over)(k, c + 2).start()
                if k < 3:
                    up(own.at[c + 2, device % 2], k, c + 2).start()

    def settle(c):
        @pl.when(me >= 2)
        def _():
            for k in range(2):
                aside(k, c).wait_recv()

        @pl.when((me == 4) | (me == 5))
        def _():
            aside(2, c).wait_recv()

    def compute(c):
        sides = []
        head = 2 * lax.rem(c, 2) + lax.div(c, 2)
        for i in range(2):
            parts = [pre[HK * i + head], own[c, i]]
            slots = [held[c, k, i].astype(F32) for k in range(4)]
            for w in weight:
                parts.append((w[0] * slots[0] + w[1] * slots[1] + w[2] * slots[2] + w[3] * slots[3]).astype(BF16))
            sides.append(jnp.concatenate(parts, axis=0))
        columns = head_columns(c)
        out[:, columns], d_query[:, columns], grad_keys, grad_values = attend_group(
            query[:, columns], d_out[:, columns], sides[0], sides[1], prefix_rows, lengths[0, me],
            [length for _, length, _ in found],
        )
        for i, grads in enumerate((grad_keys, grad_values)):
            d_pre[HK * i + head] = grads[:prefix_rows].astype(BF16)
            d_own[c, i] = grads[prefix_rows:prefix_rows + block]
            pieces = [grads[prefix_rows + s * block:prefix_rows + (s + 1) * block] for s in range(1, SLOTS + 1)]
            for k in range(4):
                mine[c, k, i] = weight[0][k] * pieces[0] + weight[1][k] * pieces[1] + weight[2][k] * pieces[2]

        for store in stores(c):
            store.start()

        @pl.when(me >= 2)
        def _():
            for k in range(2):
                other[c, k] = mine[c, k, 1 - side].astype(BF16)
                cross(k, c).start()

        @pl.when((me == 4) | (me == 5))
        def _():
            other[c, 2] = mine[c, 2, 1 - side].astype(BF16)
            cross(2, c).start()

        @pl.when(me == 7)
        def _():
            to_beside[c] = mine[c, 3].astype(BF16)
            back(c).start()

        for i in range(2):
            to = 2 * i + lax.rem(c, 2)

            @pl.when(smp != to)
            def _():
                p_copy(to, lax.rem(to - smp + 4, 4), lax.div(c, 2)).start()

    def shared(c, index):
        near, far = below[c, 0].astype(F32), below[c, 1].astype(F32)
        return jnp.where(first == index, 1.0, 0.0) * near + jnp.where(second == index, 1.0, 0.0) * far

    def add_down(c):
        def send_sum(k, more):
            cross(k, c).wait_recv()
            total = mine[c, k, side] + other_in[c, k].astype(F32)
            if more is not None:
                total += more
            sums[c, k] = total.astype(BF16)
            down(k, c).start()

        @pl.when(me >= 6)
        def _():
            for k in range(2):
                send_sum(k, None)

        @pl.when((me == 4) | (me == 5))
        def _():
            for k in range(2):
                down(k, c).wait_recv()
            for k in range(3):
                send_sum(k, shared(c, k))

        @pl.when(me == 4)
        def _():
            to_beside[c, 0] = (mine[c, 3, 0] + shared(c, 5)).astype(BF16)
            back_keys(c).start()

        @pl.when(me == 5)
        def _():
            to_beside[c, 0] = mine[c, 3, 0].astype(BF16)
            to_beside[c, 1] = (mine[c, 3, 1] + shared(c, 4)).astype(BF16)
            back(c).start()

        @pl.when((me == 2) | (me == 3))
        def _():
            for k in range(2):
                down(k, c).wait_recv()
                send_sum(k, below[c, k].astype(F32))
            down(2, c).wait_recv()

        @pl.when(me == 3)
        def _():
            to_beside[c, 0] = mine[c, 2, 0].astype(BF16)
            to_beside[c, 1] = (mine[c, 2, 1] + below[c, 2].astype(F32)).astype(BF16)
            back(c).start()

        @pl.when(me < 2)
        def _():
            for k in range(2):
                down(k, c).wait_recv()

        @pl.when(me == 0)
        def _():
            to_beside[c, 0] = (mine[c, 1, 0] + below[c, 1].astype(F32)).astype(BF16)
            back_keys(c).start()

        @pl.when(me == 1)
        def _():
            to_beside[c, 0] = mine[c, 0, 0].astype(BF16)
            to_beside[c, 1] = (mine[c, 0, 1] + below[c, 0].astype(F32)).astype(BF16)
            back(c).start()

    def sum_prefix():
        for d in range(1, smp_size):
            for i in range(2):
                p_after(d, i).wait_recv()
        total = d_pre[my_columns].astype(F32)
        for d in range(1, smp_size):
            total += p_in[d - 1].astype(F32)
        p_sum[...] = total
        p_low[...] = total.astype(BF16)
        for d in range(1, ctx_size):
            q_copy(d).start()

    down_lag = jnp.where(me >= 6, 2, jnp.where(me >= 4, 3, 4))
    prefix_step = jnp.where((me >= 4) & (me < 6), HK + 2, HK + 1)

    @pl.loop(0, 2 * HK)
    def _(t):
        @pl.when(t < HK)
        def _():
            forward(t)

        @pl.when(t == 1)
        def _():
            for load in loads:
                load.wait()
            for d in range(1, smp_size):
                b_copy(d, 0).wait_recv()

        @pl.when(t == 3)
        def _():
            for d in range(1, smp_size):
                b_copy(d, 1).wait_recv()

        @pl.when((t >= 1) & (t < HK + 1))
        def _():
            settle(t - 1)
            compute(t - 1)

        @pl.when((t >= down_lag) & (t < HK + down_lag))
        def _():
            add_down(t - down_lag)

        @pl.when(t == prefix_step)
        def _():
            sum_prefix()

    for device in (0, 1, 2, 4, 5, 6):
        @pl.when(me == device)
        def _():
            for c in range(HK):
                if device in (1, 5):
                    back_keys(c).wait_recv()
                else:
                    back(c).wait_recv()
                for i in range(2):
                    total = d_own[c, i]
                    if i == 0 or device not in (1, 5):
                        total += beside_in[c, i].astype(F32)
                    if i == device % 2 and device < 3:
                        total += below[c, device].astype(F32)
                    elif i == device % 2 and device < 6:
                        total += shared(c, device)
                    d_branch[:, block_columns(HK * i + HEAD_ORDER[c])] = total.astype(BF16)

    @pl.when((me == 3) | (me == 7))
    def _():
        for c in range(HK):
            for i in range(2):
                d_branch[:, block_columns(HK * i + HEAD_ORDER[c])] = d_own[c, i].astype(BF16)

    total = p_sum[:, my_rows]
    for d in range(1, ctx_size):
        q_copy(d).wait_recv()
        total += q_in[d - 1].astype(F32)
    for i in range(2):
        d_prefix[:, i * HD:(i + 1) * HD] = total[i].astype(BF16)

    for d in range(1, ctx_size):
        a_copy(d).wait_send()
        q_copy(d).wait_send()
    for d in range(1, smp_size):
        for i in range(2):
            b_copy(d, i).wait_send()
            p_after(d, i).wait_send()
    for c in range(HK):
        for store in stores(c):
            store.wait()

    def drain(active, copies):
        @pl.when(active)
        def _():
            for c in range(HK):
                for copy in copies:
                    copy(c).wait_send()

    def on(copy, k):
        return lambda c: copy(k, c)

    def climb(k):
        return lambda c: up(stage.at[c, 0], k, c)

    even = (me == 0) | (me == 2) | (me == 4) | (me == 6)
    drain(even, (on(over, 0),))
    drain((me == 1) | (me == 5), (on(over_keys, 1),))
    drain(me < 6, (climb(0), climb(1)))
    drain((me == 2) | (me == 3), (climb(2),))
    drain(me >= 2, (on(aside, 0), on(aside, 1), on(cross, 0), on(cross, 1), on(down, 0), on(down, 1)))
    drain((me == 4) | (me == 5), (on(aside, 2), on(cross, 2), on(down, 2)))
    drain(side == 1, (back,))
    drain((me == 0) | (me == 4), (back_keys,))


def hand_over_kernel(a, b, c, d, a_out, b_out, c_out, d_out):
    for src, dst in ((a, a_out), (b, b_out), (c, c_out), (d, d_out)):
        dst[...] = src[...]


def per_device(query, d_out, branch_kv, prefix_kv, parents, lengths):
    ctx_size, smp_size = lax.axis_size("ctx"), lax.axis_size("smp")
    p_rows, p_cols = prefix_kv.shape
    if parents.shape[1] != 8 or ctx_size != 8 or p_cols != 2 * HD or smp_size != 4:
        return per_device_general(query, d_out, branch_kv, prefix_kv, parents, lengths)
    block, width = query.shape[1:]
    prefix_rows = p_rows * ctx_size
    smem = pl.BlockSpec(memory_space=pltpu.SMEM)
    vmem = pl.BlockSpec(memory_space=pltpu.VMEM)
    dma = pltpu.SemaphoreType.DMA
    anywhere = pl.BlockSpec(memory_space=pl.ANY)
    half = (block, HD)
    pair = (2,) + half
    results = pl.pallas_call(
        functools.partial(tree_kernel, ctx_size, smp_size),
        in_specs=[smem, smem, anywhere, anywhere, vmem, vmem],
        out_specs=[anywhere, anywhere, vmem, vmem],
        out_shape=[
            jax.ShapeDtypeStruct((block, width), BF16),
            jax.ShapeDtypeStruct((block, width), BF16),
            jax.ShapeDtypeStruct(branch_kv.shape[1:], BF16),
            jax.ShapeDtypeStruct(prefix_kv.shape, BF16),
        ],
        scratch_shapes=[
            pltpu.VMEM((block, width), BF16),
            pltpu.VMEM((block, width), BF16),
            pltpu.VMEM((block, width), BF16),
            pltpu.VMEM((block, width), BF16),
            dma((2,)), dma((2, HK)),
            pltpu.VMEM((HK,) + pair, BF16),
            pltpu.VMEM((HK, 4) + pair, BF16),
            pltpu.VMEM((HK, 2) + half, BF16),
            pltpu.VMEM((2, p_rows, HD), BF16),
            pltpu.VMEM((2 * HK, prefix_rows, HD), BF16),
            pltpu.VMEM((HK, 4) + pair, F32),
            pltpu.VMEM((HK,) + pair, F32),
            pltpu.VMEM((HK, 3) + half, BF16),
            pltpu.VMEM((HK, 3) + half, BF16),
            pltpu.VMEM((HK,) + pair, BF16),
            pltpu.VMEM((HK, 3) + half, BF16),
            pltpu.VMEM((HK, 3) + half, BF16),
            pltpu.VMEM((HK,) + pair, BF16),
            pltpu.VMEM((2 * HK, prefix_rows, HD), BF16),
            pltpu.VMEM((smp_size - 1, 2, prefix_rows, HD), BF16),
            pltpu.VMEM((2, prefix_rows, HD), F32),
            pltpu.VMEM((2, prefix_rows, HD), BF16),
            pltpu.VMEM((ctx_size - 1, 2, p_rows, HD), BF16),
            dma((3, HK)), dma((3, HK)), dma((HK,)), dma((HK,)), dma((3, HK)), dma((3, HK)),
            dma((ctx_size - 1,)), dma((ctx_size - 1,)), dma((smp_size - 1, 2)), dma((smp_size - 1, 2)),
            dma((3, HK)), dma((3, HK)), dma((3, HK)), dma((3, HK)), dma((HK,)), dma((HK,)),
            dma((smp_size - 1, 2)), dma((smp_size - 1, 2)), dma((ctx_size - 1,)), dma((ctx_size - 1,)),
        ],
        compiler_params=pltpu.CompilerParams(
            collective_id=0, has_side_effects=True, vmem_limit_bytes=VMEM_LIMIT
        ),
        name="tree_attention",
    )(parents, lengths, query[0], d_out[0], branch_kv[0], prefix_kv)
    rows = [pl.BlockSpec((x.shape[0] // HK, x.shape[1]), lambda r: (r, 0)) for x in results[:3]]
    rows.append(pl.BlockSpec(results[3].shape, lambda r: (0, 0)))
    out, d_query, d_branch, d_prefix = pl.pallas_call(
        hand_over_kernel,
        grid=(HK,),
        in_specs=rows,
        out_specs=rows,
        out_shape=[jax.ShapeDtypeStruct(x.shape, x.dtype) for x in results],
        name="hand_over",
    )(*results)
    return out[None], d_query[None], d_branch[None], d_prefix


def solution(mesh):
    return jax.shard_map(
        per_device,
        mesh=mesh,
        in_specs=(
            P("smp", "ctx", None),
            P("smp", "ctx", None),
            P("smp", "ctx", None),
            P("ctx", "smp"),
            P("smp", None),
            P("smp", None),
        ),
        out_specs=(
            P("smp", "ctx", None),
            P("smp", "ctx", None),
            P("smp", "ctx", None),
            P("ctx", "smp"),
        ),
        check_vma=False,
    )
```

```python
import functools
import math

import jax
import jax.numpy as jnp
from jax import lax
from jax.experimental import pallas as pl
from jax.experimental.pallas import tpu as pltpu
from jax.sharding import PartitionSpec as P

HK = 4
HD = 128
PARTS = 2
F32 = jnp.float32
BF16 = jnp.bfloat16


def walk_up(parents, lengths, start, count):
    found = []
    at = start
    for _ in range(count):
        up = parents[0, jnp.maximum(at, 0)]
        at = jnp.where(at >= 0, up, -1)
        held = jnp.maximum(at, 0)
        found.append((held, jnp.where(at >= 0, lengths[0, held], 0), at >= 0))
    return found


def attend_group(query, d_out, keys, values, prefix_rows, own_length, slot_lengths):
    block = query.shape[0]
    group = query.shape[1] // HD
    scale = HD ** -0.5
    to_exp2 = scale * math.log2(math.e)
    place = lax.broadcasted_iota(jnp.int32, (block, 1), 0)
    grad_live = jnp.where(place < own_length, d_out, jnp.zeros_like(d_out))

    def heads(x):
        return [x[:, h * HD:(h + 1) * HD] for h in range(group)]

    row = lax.broadcasted_iota(jnp.int32, (block, block), 1)
    key = lax.broadcasted_iota(jnp.int32, (block, block), 0)
    part = group // PARTS
    own_bias = jnp.where((key < own_length) & (key <= row), 0.0, -jnp.inf)
    own_bias = jnp.concatenate([own_bias] * part, axis=1)
    slot_bias = [jnp.where(place < length, 0.0, -jnp.inf) for length in slot_lengths]
    live = lax.broadcasted_iota(jnp.int32, (1, block), 1) < own_length
    live = jnp.concatenate([jnp.where(live, 1.0, 0.0)] * part, axis=1)

    def softmax(scores):
        parts = [scores[:prefix_rows], scores[prefix_rows:prefix_rows + block] + own_bias]
        for s, bias in enumerate(slot_bias):
            first = prefix_rows + (s + 1) * block
            parts.append(scores[first:first + block] + bias)
        scores = jnp.concatenate(parts, axis=0)
        top = jnp.max(scores, axis=0, keepdims=True) * to_exp2
        exponent = jnp.exp2(scores * to_exp2 - top)
        return exponent * (1.0 / jnp.sum(exponent, axis=0, keepdims=True))

    def dot(x, y, over):
        return lax.dot_general(x, y, (over, ((), ())), preferred_element_type=F32)

    all_queries, all_grads = heads(query), heads(grad_live)
    taken = [slice(p * part, (p + 1) * part) for p in range(PARTS)]
    query_rows = [jnp.concatenate(all_queries[t], axis=0) for t in taken]
    grad_rows = [jnp.concatenate(all_grads[t], axis=0) for t in taken]
    grad_cols = [jnp.concatenate([h.T for h in all_grads[t]], axis=1) for t in taken]
    scores = [dot(keys, q, ((1,), (1,))) for q in query_rows]
    out, d_query, grad_keys, grad_values = [], [], 0.0, 0.0
    for p in range(PARTS):
        grad_probs = dot(values, grad_cols[p], ((1,), (0,)))
        probs = softmax(scores[p])
        probs_low = probs.astype(BF16)
        attended = (dot(values, probs_low, ((0,), (0,))) * live).astype(BF16)
        delta = jnp.sum(grad_cols[p].astype(F32) * attended.astype(F32), axis=0, keepdims=True)
        grad_scores = (probs * (grad_probs - delta)).astype(BF16)
        grad_query = (dot(keys, grad_scores, ((0,), (0,))) * scale).astype(BF16)
        grad_keys += dot(grad_scores, query_rows[p], ((1,), (0,)))
        grad_values += dot(probs_low, grad_rows[p], ((1,), (0,)))
        out += [h.T for h in heads_across(attended, block)]
        d_query += [h.T for h in heads_across(grad_query, block)]
    return jnp.concatenate(out, axis=1), jnp.concatenate(d_query, axis=1), grad_keys * scale, grad_values


def heads_across(x, block):
    return [x[:, h * block:(h + 1) * block] for h in range(x.shape[1] // block)]


def attend_kernel(
    slots, parents, lengths, query, d_out, prefix_k, prefix_v, branch_k, branch_v,
    out, d_query, d_prefix_k, d_prefix_v, d_branch_k, d_branch_v,
):
    me = lax.axis_index("ctx")
    prefix_rows = prefix_k.shape[0]
    block = query.shape[0]
    found = walk_up(parents, lengths, me, slots)
    blocks = [me] + [index for index, _, _ in found]
    keys = jnp.concatenate([prefix_k[...]] + [branch_k[b] for b in blocks], axis=0)
    values = jnp.concatenate([prefix_v[...]] + [branch_v[b] for b in blocks], axis=0)
    out[...], d_query[...], grad_keys, grad_values = attend_group(
        query[...], d_out[...], keys, values, prefix_rows, lengths[0, me], [length for _, length, _ in found]
    )
    for grads, to_prefix, to_branch in ((grad_keys, d_prefix_k, d_branch_k), (grad_values, d_prefix_v, d_branch_v)):
        to_prefix[...] = grads[:prefix_rows]
        to_branch[...] = jnp.zeros_like(to_branch)
        for s, b in enumerate(blocks):
            first = prefix_rows + s * block
            piece = grads[first:first + block]
            if s == 0:
                to_branch[b] = piece
            else:
                @pl.when(found[s - 1][2])
                def _():
                    to_branch[b] = piece


def per_device_general(query, d_out, branch_kv, prefix_kv, parents, lengths):
    num_blocks = parents.shape[1]
    slots = max(4, num_blocks // 4) - 1
    block = query.shape[1]
    width = query.shape[2]
    with_features = lax.all_gather(prefix_kv, "smp", axis=1, tiled=True)
    prefix_all = lax.all_gather(with_features, "ctx", axis=0, tiled=True)
    prefix_rows, features = prefix_all.shape
    all_blocks = lax.all_gather(branch_kv[0], "ctx", axis=0)
    group_width = width // HK
    smem = pl.BlockSpec(memory_space=pltpu.SMEM)
    heads = pl.BlockSpec((block, group_width), lambda g: (0, g))
    prefix_k = pl.BlockSpec((prefix_rows, HD), lambda g: (0, g))
    prefix_v = pl.BlockSpec((prefix_rows, HD), lambda g: (0, g + HK))
    branch_k = pl.BlockSpec((num_blocks, block, HD), lambda g: (0, 0, g))
    branch_v = pl.BlockSpec((num_blocks, block, HD), lambda g: (0, 0, g + HK))
    grad_prefix = jax.ShapeDtypeStruct((prefix_rows, features // 2), F32)
    grad_branch = jax.ShapeDtypeStruct((num_blocks, block, features // 2), F32)
    out, d_query, dpk, dpv, dbk, dbv = pl.pallas_call(
        functools.partial(attend_kernel, slots),
        grid=(HK,),
        in_specs=[smem, smem, heads, heads, prefix_k, prefix_v, branch_k, branch_v],
        out_specs=[heads, heads, prefix_k, prefix_k, branch_k, branch_k],
        out_shape=[
            jax.ShapeDtypeStruct((block, width), BF16),
            jax.ShapeDtypeStruct((block, width), BF16),
            grad_prefix, grad_prefix, grad_branch, grad_branch,
        ],
        compiler_params=pltpu.CompilerParams(vmem_limit_bytes=56 * 1024 * 1024),
    )(parents, lengths, query[0], d_out[0], prefix_all, prefix_all, all_blocks, all_blocks)
    spread = jnp.concatenate([dbk, dbv], axis=2).reshape(num_blocks * block, features)
    grad_branch = lax.psum_scatter(spread, "ctx", scatter_dimension=0, tiled=True)
    grad_rows = lax.psum_scatter(jnp.concatenate([dpk, dpv], axis=1), "ctx", scatter_dimension=0, tiled=True)
    grad_prefix_out = lax.psum_scatter(grad_rows, "smp", scatter_dimension=1, tiled=True)
    return out[None], d_query[None], grad_branch.astype(BF16)[None], grad_prefix_out.astype(BF16)


SLOTS = 3
MESH = pl.DeviceIdType.MESH
VMEM_LIMIT = 56 * 1024 * 1024


def greet(ctx_size, smp_size, me, smp):
    barrier = pltpu.get_barrier_semaphore()
    for d in range(1, ctx_size):
        pl.semaphore_signal(barrier, inc=1, device_id={"ctx": lax.rem(me + d, ctx_size)}, device_id_type=MESH)
    for d in range(1, smp_size):
        pl.semaphore_signal(barrier, inc=1, device_id={"smp": lax.rem(smp + d, smp_size)}, device_id_type=MESH)
    pl.semaphore_wait(barrier, ctx_size + smp_size - 2)


def remote(src, dst, send, recv, to):
    return pltpu.make_async_remote_copy(
        src_ref=src, dst_ref=dst, send_sem=send, recv_sem=recv, device_id=to, device_id_type=MESH
    )


HEAD_ORDER = (0, 2, 1, 3)


def block_columns(i):
    return slice(i * HD, (i + 1) * HD)


def tree_kernel(
    ctx_size, smp_size, parents, lengths, query_far, d_out_far, branch, prefix,
    out_far, d_query_far, d_branch, d_prefix,
    query, d_out, out, d_query, load_sem, store_sem,
    own, held, stage, pre_own, pre, mine, d_own, other, sums, to_beside, below, other_in, beside_in,
    d_pre, p_in, p_sum, p_low, q_in,
    up_send, up_recv, over_send, over_recv, aside_send, aside_recv, a_send, a_recv, b_send, b_recv,
    down_send, down_recv, cross_send, cross_recv, back_send, back_recv, p_send, p_recv, q_send, q_recv,
):
    me, smp = lax.axis_index("ctx"), lax.axis_index("smp")
    side = lax.rem(me, 2)
    beside = me + 1 - 2 * side
    block = branch.shape[0]
    group_width = query.shape[1] // HK
    p_rows = prefix.shape[0]
    prefix_rows = pre.shape[1]
    loads = [
        pltpu.make_async_copy(query_far, query, load_sem.at[0]), pltpu.make_async_copy(d_out_far, d_out, load_sem.at[1])
    ]
    for load in loads:
        load.start()
    greet(ctx_size, smp_size, me, smp)

    def up(src, k, c):
        return remote(src, held.at[c, k, side], up_send.at[k, c], up_recv.at[k, c], {"ctx": me + 2})

    def aside(k, c):
        half = held.at[c, k, side]
        return remote(half, half, aside_send.at[k, c], aside_recv.at[k, c], {"ctx": beside})

    def over(k, c):
        return remote(own.at[c], held.at[c, k], over_send.at[c], over_recv.at[c], {"ctx": beside})

    def over_keys(k, c):
        return remote(own.at[c, 0], held.at[c, k, 0], over_send.at[c], over_recv.at[c], {"ctx": beside})

    def down(k, c):
        return remote(sums.at[c, k], below.at[c, k], down_send.at[k, c], down_recv.at[k, c], {"ctx": me - 2})

    def cross(k, c):
        return remote(other.at[c, k], other_in.at[c, k], cross_send.at[k, c], cross_recv.at[k, c], {"ctx": beside})

    def back(c):
        return remote(to_beside.at[c], beside_in.at[c], back_send.at[c], back_recv.at[c], {"ctx": beside})

    def back_keys(c):
        return remote(to_beside.at[c, 0], beside_in.at[c, 0], back_send.at[c], back_recv.at[c], {"ctx": beside})

    my_rows = pl.ds(pl.multiple_of(me * p_rows, p_rows), p_rows)
    my_columns = pl.ds(2 * smp, 2)

    def a_copy(d):
        return remote(
            pre_own, pre.at[my_columns, my_rows], a_send.at[d - 1], a_recv.at[d - 1], {"ctx": lax.rem(me + d, ctx_size)}
        )

    def b_copy(d, i):
        columns = pre.at[2 * smp + i]
        return remote(columns, columns, b_send.at[d - 1, i], b_recv.at[d - 1, i], {"smp": lax.rem(smp + d, smp_size)})

    def p_copy(to, d, i):
        return remote(
            d_pre.at[2 * to + i], p_in.at[d - 1, i], p_send.at[d - 1, i], p_recv.at[d - 1, i], {"smp": to}
        )

    def p_after(d, i):
        return p_copy(lax.rem(smp + d, smp_size), d, i)

    def head_columns(c):
        head = 2 * lax.rem(c, 2) + lax.div(c, 2)
        return pl.ds(pl.multiple_of(head * group_width, group_width), group_width)

    def stores(c):
        columns = head_columns(c)
        return [
            pltpu.make_async_copy(src.at[:, columns], dst.at[:, columns], store_sem.at[i, c])
            for i, (src, dst) in enumerate(((out, out_far), (d_query, d_query_far)))
        ]

    def q_copy(d):
        to = lax.rem(me + d, ctx_size)
        rows = pl.ds(pl.multiple_of(to * p_rows, p_rows), p_rows)
        return remote(p_low.at[:, rows], q_in.at[d - 1], q_send.at[d - 1], q_recv.at[d - 1], {"ctx": to})

    for i in range(2):
        pre_own[i] = prefix[:, i * HD:(i + 1) * HD]
        pre[2 * smp + i, my_rows] = prefix[:, i * HD:(i + 1) * HD]
    for d in range(1, ctx_size):
        a_copy(d).start()
    for c in range(HK):
        for i in range(2):
            own[c, i] = branch[:, block_columns(HK * i + HEAD_ORDER[c])]
    for device, k in ((0, 0), (1, 1), (2, 2), (4, 3), (5, 3), (6, 3)):
        @pl.when(me == device)
        def _():
            for c in range(2):
                (over_keys if device in (1, 5) else over)(k, c).start()
                if k < 3:
                    up(own.at[c, device % 2], k, c).start()
    for k, without in ((0, me == 0), (1, me < 2), (2, (me < 3) | (me > 5)), (3, (me < 5) | (me == 6))):
        @pl.when(without)
        def _():
            for c in range(HK):
                held[c, k, 1] = jnp.zeros((block, HD), BF16)
    for k, without in ((0, me == 0), (1, me == 1), (2, (me < 3) | (me > 5)), (3, (me < 4) | (me == 6))):
        @pl.when(without)
        def _():
            for c in range(HK):
                held[c, k, 0] = jnp.zeros((block, HD), BF16)
    for d in range(1, ctx_size):
        a_copy(d).wait_recv()
    for i in range(2):
        for d in range(1, smp_size):
            b_copy(d, i).start()

    first = parents[0, 6]
    second = jnp.where(first >= 0, parents[0, jnp.maximum(first, 0)], -1)
    found = walk_up(parents, lengths, me, SLOTS)
    weight = []
    for s, (index, _, there) in enumerate(found):
        place = jnp.where(me < 6, jnp.minimum(index, 3), jnp.where(me == 6, s, 3 if s == 0 else s - 1))
        weight.append([jnp.where(there & (place == k), 1.0, 0.0) for k in range(4)])

    def forward(c):
        def pass_on(k):
            up(held.at[c, k, side], k, c).wait_recv()
            up(held.at[c, k, side], k, c).start()
            aside(k, c).start()

        @pl.when(me == 0)
        def _():
            over_keys(1, c).wait_recv()
            up(held.at[c, 1, 0], 1, c).start()

        @pl.when(me == 1)
        def _():
            over(0, c).wait_recv()
            up(held.at[c, 0, 1], 0, c).start()

        @pl.when(me == 2)
        def _():
            pass_on(0)
            pass_on(1)

        @pl.when(me == 3)
        def _():
            over(2, c).wait_recv()
            up(held.at[c, 2, 1], 2, c).start()
            pass_on(1)
            pass_on(0)

        @pl.when((me == 4) | (me == 5))
        def _():
            for k in range(3):
                up(held.at[c, k, side], k, c).wait_recv()
                aside(k, c).start()

        @pl.when(me == 4)
        def _():
            over_keys(3, c).wait_recv()

        @pl.when(me == 5)
        def _():
            over(3, c).wait_recv()

        @pl.when((me == 4) | (me == 5))
        def _():
            for k, want in enumerate((first, second)):
                total = jnp.where(want == me, 1.0, 0.0) * own[c, side].astype(F32)
                for slot, index in ((0, 0), (1, 1), (2, 2), (3, beside)):
                    total += jnp.where(want == index, 1.0, 0.0) * held[c, slot, side].astype(F32)
                stage[c, k] = total.astype(BF16)
                up(stage.at[c, k], k, c).start()

        @pl.when(me >= 6)
        def _():
            for k in range(2):
                up(held.at[c, k, side], k, c).wait_recv()
                aside(k, c).start()

        @pl.when(me == 7)
        def _():
            over(3, c).wait_recv()

        for device, k in ((0, 0), (1, 1), (2, 2), (4, 3), (5, 3), (6, 3)):
            @pl.when((me == device) & (c < HK - 2))
            def _():
                (over_keys if device in (1, 5) else over)(k, c + 2).start()
                if k < 3:
                    up(own.at[c + 2, device % 2], k, c + 2).start()

    def settle(c):
        @pl.when(me >= 2)
        def _():
            for k in range(2):
                aside(k, c).wait_recv()

        @pl.when((me == 4) | (me == 5))
        def _():
            aside(2, c).wait_recv()

    def compute(c):
        sides = []
        head = 2 * lax.rem(c, 2) + lax.div(c, 2)
        for i in range(2):
            parts = [pre[HK * i + head], own[c, i]]
            slots = [held[c, k, i].astype(F32) for k in range(4)]
            for w in weight:
                parts.append((w[0] * slots[0] + w[1] * slots[1] + w[2] * slots[2] + w[3] * slots[3]).astype(BF16))
            sides.append(jnp.concatenate(parts, axis=0))
        columns = head_columns(c)
        out[:, columns], d_query[:, columns], grad_keys, grad_values = attend_group(
            query[:, columns], d_out[:, columns], sides[0], sides[1], prefix_rows, lengths[0, me],
            [length for _, length, _ in found],
        )
        for i, grads in enumerate((grad_keys, grad_values)):
            d_pre[HK * i + head] = grads[:prefix_rows].astype(BF16)
            d_own[c, i] = grads[prefix_rows:prefix_rows + block]
            pieces = [grads[prefix_rows + s * block:prefix_rows + (s + 1) * block] for s in range(1, SLOTS + 1)]
            for k in range(4):
                mine[c, k, i] = weight[0][k] * pieces[0] + weight[1][k] * pieces[1] + weight[2][k] * pieces[2]

        for store in stores(c):
            store.start()

        @pl.when(me >= 2)
        def _():
            for k in range(2):
                other[c, k] = mine[c, k, 1 - side].astype(BF16)
                cross(k, c).start()

        @pl.when((me == 4) | (me == 5))
        def _():
            other[c, 2] = mine[c, 2, 1 - side].astype(BF16)
            cross(2, c).start()

        @pl.when(me == 7)
        def _():
            to_beside[c] = mine[c, 3].astype(BF16)
            back(c).start()

        for i in range(2):
            to = 2 * i + lax.rem(c, 2)

            @pl.when(smp != to)
            def _():
                p_copy(to, lax.rem(to - smp + 4, 4), lax.div(c, 2)).start()

    def shared(c, index):
        near, far = below[c, 0].astype(F32), below[c, 1].astype(F32)
        return jnp.where(first == index, 1.0, 0.0) * near + jnp.where(second == index, 1.0, 0.0) * far

    def add_down(c):
        def send_sum(k, more):
            cross(k, c).wait_recv()
            total = mine[c, k, side] + other_in[c, k].astype(F32)
            if more is not None:
                total += more
            sums[c, k] = total.astype(BF16)
            down(k, c).start()

        @pl.when(me >= 6)
        def _():
            for k in range(2):
                send_sum(k, None)

        @pl.when((me == 4) | (me == 5))
        def _():
            for k in range(2):
                down(k, c).wait_recv()
            for k in range(3):
                send_sum(k, shared(c, k))

        @pl.when(me == 4)
        def _():
            to_beside[c, 0] = (mine[c, 3, 0] + shared(c, 5)).astype(BF16)
            back_keys(c).start()

        @pl.when(me == 5)
        def _():
            to_beside[c, 0] = mine[c, 3, 0].astype(BF16)
            to_beside[c, 1] = (mine[c, 3, 1] + shared(c, 4)).astype(BF16)
            back(c).start()

        @pl.when((me == 2) | (me == 3))
        def _():
            for k in range(2):
                down(k, c).wait_recv()
                send_sum(k, below[c, k].astype(F32))
            down(2, c).wait_recv()

        @pl.when(me == 3)
        def _():
            to_beside[c, 0] = mine[c, 2, 0].astype(BF16)
            to_beside[c, 1] = (mine[c, 2, 1] + below[c, 2].astype(F32)).astype(BF16)
            back(c).start()

        @pl.when(me < 2)
        def _():
            for k in range(2):
                down(k, c).wait_recv()

        @pl.when(me == 0)
        def _():
            to_beside[c, 0] = (mine[c, 1, 0] + below[c, 1].astype(F32)).astype(BF16)
            back_keys(c).start()

        @pl.when(me == 1)
        def _():
            to_beside[c, 0] = mine[c, 0, 0].astype(BF16)
            to_beside[c, 1] = (mine[c, 0, 1] + below[c, 0].astype(F32)).astype(BF16)
            back(c).start()

    def sum_prefix():
        for d in range(1, smp_size):
            for i in range(2):
                p_after(d, i).wait_recv()
        total = d_pre[my_columns].astype(F32)
        for d in range(1, smp_size):
            total += p_in[d - 1].astype(F32)
        p_sum[...] = total
        p_low[...] = total.astype(BF16)
        for d in range(1, ctx_size):
            q_copy(d).start()

    down_lag = jnp.where(me >= 6, 2, jnp.where(me >= 4, 3, 4))
    prefix_step = jnp.where((me >= 4) & (me < 6), HK + 2, HK + 1)

    @pl.loop(0, 2 * HK)
    def _(t):
        @pl.when(t < HK)
        def _():
            forward(t)

        @pl.when(t == 1)
        def _():
            for load in loads:
                load.wait()
            for d in range(1, smp_size):
                b_copy(d, 0).wait_recv()

        @pl.when(t == 3)
        def _():
            for d in range(1, smp_size):
                b_copy(d, 1).wait_recv()

        @pl.when((t >= 1) & (t < HK + 1))
        def _():
            settle(t - 1)
            compute(t - 1)

        @pl.when((t >= down_lag) & (t < HK + down_lag))
        def _():
            add_down(t - down_lag)

        @pl.when(t == prefix_step)
        def _():
            sum_prefix()

    for device in (0, 1, 2, 4, 5, 6):
        @pl.when(me == device)
        def _():
            for c in range(HK):
                if device in (1, 5):
                    back_keys(c).wait_recv()
                else:
                    back(c).wait_recv()
                for i in range(2):
                    total = d_own[c, i]
                    if i == 0 or device not in (1, 5):
                        total += beside_in[c, i].astype(F32)
                    if i == device % 2 and device < 3:
                        total += below[c, device].astype(F32)
                    elif i == device % 2 and device < 6:
                        total += shared(c, device)
                    d_branch[:, block_columns(HK * i + HEAD_ORDER[c])] = total.astype(BF16)

    @pl.when((me == 3) | (me == 7))
    def _():
        for c in range(HK):
            for i in range(2):
                d_branch[:, block_columns(HK * i + HEAD_ORDER[c])] = d_own[c, i].astype(BF16)

    total = p_sum[:, my_rows]
    for d in range(1, ctx_size):
        q_copy(d).wait_recv()
        total += q_in[d - 1].astype(F32)
    for i in range(2):
        d_prefix[:, i * HD:(i + 1) * HD] = total[i].astype(BF16)

    for d in range(1, ctx_size):
        a_copy(d).wait_send()
        q_copy(d).wait_send()
    for d in range(1, smp_size):
        for i in range(2):
            b_copy(d, i).wait_send()
            p_after(d, i).wait_send()
    for c in range(HK):
        for store in stores(c):
            store.wait()

    def drain(active, copies):
        @pl.when(active)
        def _():
            for c in range(HK):
                for copy in copies:
                    copy(c).wait_send()

    def on(copy, k):
        return lambda c: copy(k, c)

    def climb(k):
        return lambda c: up(stage.at[c, 0], k, c)

    even = (me == 0) | (me == 2) | (me == 4) | (me == 6)
    drain(even, (on(over, 0),))
    drain((me == 1) | (me == 5), (on(over_keys, 1),))
    drain(me < 6, (climb(0), climb(1)))
    drain((me == 2) | (me == 3), (climb(2),))
    drain(me >= 2, (on(aside, 0), on(aside, 1), on(cross, 0), on(cross, 1), on(down, 0), on(down, 1)))
    drain((me == 4) | (me == 5), (on(aside, 2), on(cross, 2), on(down, 2)))
    drain(side == 1, (back,))
    drain((me == 0) | (me == 4), (back_keys,))


def hand_over_kernel(a, b, c, d, a_out, b_out, c_out, d_out):
    for src, dst in ((a, a_out), (b, b_out), (c, c_out), (d, d_out)):
        dst[...] = src[...]


def per_device(query, d_out, branch_kv, prefix_kv, parents, lengths):
    ctx_size, smp_size = lax.axis_size("ctx"), lax.axis_size("smp")
    p_rows, p_cols = prefix_kv.shape
    if parents.shape[1] != 8 or ctx_size != 8 or p_cols != 2 * HD or smp_size != 4:
        return per_device_general(query, d_out, branch_kv, prefix_kv, parents, lengths)
    block, width = query.shape[1:]
    prefix_rows = p_rows * ctx_size
    smem = pl.BlockSpec(memory_space=pltpu.SMEM)
    vmem = pl.BlockSpec(memory_space=pltpu.VMEM)
    dma = pltpu.SemaphoreType.DMA
    anywhere = pl.BlockSpec(memory_space=pl.ANY)
    half = (block, HD)
    pair = (2,) + half
    results = pl.pallas_call(
        functools.partial(tree_kernel, ctx_size, smp_size),
        in_specs=[smem, smem, anywhere, anywhere, vmem, vmem],
        out_specs=[anywhere, anywhere, vmem, vmem],
        out_shape=[
            jax.ShapeDtypeStruct((block, width), BF16),
            jax.ShapeDtypeStruct((block, width), BF16),
            jax.ShapeDtypeStruct(branch_kv.shape[1:], BF16),
            jax.ShapeDtypeStruct(prefix_kv.shape, BF16),
        ],
        scratch_shapes=[
            pltpu.VMEM((block, width), BF16),
            pltpu.VMEM((block, width), BF16),
            pltpu.VMEM((block, width), BF16),
            pltpu.VMEM((block, width), BF16),
            dma((2,)), dma((2, HK)),
            pltpu.VMEM((HK,) + pair, BF16),
            pltpu.VMEM((HK, 4) + pair, BF16),
            pltpu.VMEM((HK, 2) + half, BF16),
            pltpu.VMEM((2, p_rows, HD), BF16),
            pltpu.VMEM((2 * HK, prefix_rows, HD), BF16),
            pltpu.VMEM((HK, 4) + pair, F32),
            pltpu.VMEM((HK,) + pair, F32),
            pltpu.VMEM((HK, 3) + half, BF16),
            pltpu.VMEM((HK, 3) + half, BF16),
            pltpu.VMEM((HK,) + pair, BF16),
            pltpu.VMEM((HK, 3) + half, BF16),
            pltpu.VMEM((HK, 3) + half, BF16),
            pltpu.VMEM((HK,) + pair, BF16),
            pltpu.VMEM((2 * HK, prefix_rows, HD), BF16),
            pltpu.VMEM((smp_size - 1, 2, prefix_rows, HD), BF16),
            pltpu.VMEM((2, prefix_rows, HD), F32),
            pltpu.VMEM((2, prefix_rows, HD), BF16),
            pltpu.VMEM((ctx_size - 1, 2, p_rows, HD), BF16),
            dma((3, HK)), dma((3, HK)), dma((HK,)), dma((HK,)), dma((3, HK)), dma((3, HK)),
            dma((ctx_size - 1,)), dma((ctx_size - 1,)), dma((smp_size - 1, 2)), dma((smp_size - 1, 2)),
            dma((3, HK)), dma((3, HK)), dma((3, HK)), dma((3, HK)), dma((HK,)), dma((HK,)),
            dma((smp_size - 1, 2)), dma((smp_size - 1, 2)), dma((ctx_size - 1,)), dma((ctx_size - 1,)),
        ],
        compiler_params=pltpu.CompilerParams(
            collective_id=0, has_side_effects=True, vmem_limit_bytes=VMEM_LIMIT
        ),
        name="tree_attention",
    )(parents, lengths, query[0], d_out[0], branch_kv[0], prefix_kv)
    rows = [pl.BlockSpec((x.shape[0] // 2, x.shape[1]), lambda r: (r, 0)) for x in results[:3]]
    rows.append(pl.BlockSpec(results[3].shape, lambda r: (0, 0)))
    out, d_query, d_branch, d_prefix = pl.pallas_call(
        hand_over_kernel,
        grid=(2,),
        in_specs=rows,
        out_specs=rows,
        out_shape=[jax.ShapeDtypeStruct(x.shape, x.dtype) for x in results],
        name="hand_over",
    )(*results)
    return out[None], d_query[None], d_branch[None], d_prefix


def solution(mesh):
    return jax.shard_map(
        per_device,
        mesh=mesh,
        in_specs=(
            P("smp", "ctx", None),
            P("smp", "ctx", None),
            P("smp", "ctx", None),
            P("ctx", "smp"),
            P("smp", None),
            P("smp", None),
        ),
        out_specs=(
            P("smp", "ctx", None),
            P("smp", "ctx", None),
            P("smp", "ctx", None),
            P("ctx", "smp"),
        ),
        check_vma=False,
    )
```

```python
import functools
import math

import jax
import jax.numpy as jnp
from jax import lax
from jax.experimental import pallas as pl
from jax.experimental.pallas import tpu as pltpu
from jax.sharding import PartitionSpec as P

HK = 4
HD = 128
F32 = jnp.float32
BF16 = jnp.bfloat16


def walk_up(parents, lengths, start, count):
    found = []
    at = start
    for _ in range(count):
        up = parents[0, jnp.maximum(at, 0)]
        at = jnp.where(at >= 0, up, -1)
        held = jnp.maximum(at, 0)
        found.append((held, jnp.where(at >= 0, lengths[0, held], 0), at >= 0))
    return found


def attend_group(query, d_out, keys, values, prefix_rows, own_length, slot_lengths):
    block = query.shape[0]
    group = query.shape[1] // HD
    scale = HD ** -0.5
    to_exp2 = scale * math.log2(math.e)
    place = lax.broadcasted_iota(jnp.int32, (block, 1), 0)
    grad_live = jnp.where(place < own_length, d_out, jnp.zeros_like(d_out))

    def heads(x):
        return [x[:, h * HD:(h + 1) * HD] for h in range(group)]

    query_rows = jnp.concatenate(heads(query), axis=0)
    grad_rows = jnp.concatenate(heads(grad_live), axis=0)
    grad_cols = jnp.concatenate([h.T for h in heads(grad_live)], axis=1)

    scores = lax.dot_general(keys, query_rows, (((1,), (1,)), ((), ())), preferred_element_type=F32)
    row = lax.broadcasted_iota(jnp.int32, (block, block), 1)
    key = lax.broadcasted_iota(jnp.int32, (block, block), 0)
    own_bias = jnp.where((key < own_length) & (key <= row), 0.0, -jnp.inf)
    own_bias = jnp.concatenate([own_bias] * group, axis=1)
    parts = [scores[:prefix_rows], scores[prefix_rows:prefix_rows + block] + own_bias]
    for s, length in enumerate(slot_lengths):
        first = prefix_rows + (s + 1) * block
        parts.append(scores[first:first + block] + jnp.where(place < length, 0.0, -jnp.inf))
    scores = jnp.concatenate(parts, axis=0)
    top = jnp.max(scores, axis=0, keepdims=True) * to_exp2
    exponent = jnp.exp2(scores * to_exp2 - top)
    probs = exponent * (1.0 / jnp.sum(exponent, axis=0, keepdims=True))
    probs_low = probs.astype(BF16)
    attended = lax.dot_general(values, probs_low, (((0,), (0,)), ((), ())), preferred_element_type=F32)
    live = lax.broadcasted_iota(jnp.int32, (1, block), 1) < own_length
    live = jnp.concatenate([jnp.where(live, 1.0, 0.0)] * group, axis=1)
    attended = (attended * live).astype(BF16)
    delta = jnp.sum(grad_cols.astype(F32) * attended.astype(F32), axis=0, keepdims=True)
    grad_probs = jnp.dot(values, grad_cols, preferred_element_type=F32)
    grad_scores = (probs * (grad_probs - delta)).astype(BF16)
    grad_query = lax.dot_general(keys, grad_scores, (((0,), (0,)), ((), ())), preferred_element_type=F32)
    grad_query = (grad_query * scale).astype(BF16)
    grad_keys = jnp.dot(grad_scores, query_rows, preferred_element_type=F32) * scale
    grad_values = jnp.dot(probs_low, grad_rows, preferred_element_type=F32)
    return (
        jnp.concatenate([h.T for h in heads_across(attended, block)], axis=1),
        jnp.concatenate([h.T for h in heads_across(grad_query, block)], axis=1),
        grad_keys,
        grad_values,
    )


def heads_across(x, block):
    return [x[:, h * block:(h + 1) * block] for h in range(x.shape[1] // block)]


def attend_kernel(
    slots, parents, lengths, query, d_out, prefix_k, prefix_v, branch_k, branch_v,
    out, d_query, d_prefix_k, d_prefix_v, d_branch_k, d_branch_v,
):
    me = lax.axis_index("ctx")
    prefix_rows = prefix_k.shape[0]
    block = query.shape[0]
    found = walk_up(parents, lengths, me, slots)
    blocks = [me] + [index for index, _, _ in found]
    keys = jnp.concatenate([prefix_k[...]] + [branch_k[b] for b in blocks], axis=0)
    values = jnp.concatenate([prefix_v[...]] + [branch_v[b] for b in blocks], axis=0)
    out[...], d_query[...], grad_keys, grad_values = attend_group(
        query[...], d_out[...], keys, values, prefix_rows, lengths[0, me], [length for _, length, _ in found]
    )
    for grads, to_prefix, to_branch in ((grad_keys, d_prefix_k, d_branch_k), (grad_values, d_prefix_v, d_branch_v)):
        to_prefix[...] = grads[:prefix_rows]
        to_branch[...] = jnp.zeros_like(to_branch)
        for s, b in enumerate(blocks):
            first = prefix_rows + s * block
            piece = grads[first:first + block]
            if s == 0:
                to_branch[b] = piece
            else:
                @pl.when(found[s - 1][2])
                def _():
                    to_branch[b] = piece


def per_device_general(query, d_out, branch_kv, prefix_kv, parents, lengths):
    num_blocks = parents.shape[1]
    slots = max(4, num_blocks // 4) - 1
    block = query.shape[1]
    width = query.shape[2]
    with_features = lax.all_gather(prefix_kv, "smp", axis=1, tiled=True)
    prefix_all = lax.all_gather(with_features, "ctx", axis=0, tiled=True)
    prefix_rows, features = prefix_all.shape
    all_blocks = lax.all_gather(branch_kv[0], "ctx", axis=0)
    group_width = width // HK
    smem = pl.BlockSpec(memory_space=pltpu.SMEM)
    heads = pl.BlockSpec((block, group_width), lambda g: (0, g))
    prefix_k = pl.BlockSpec((prefix_rows, HD), lambda g: (0, g))
    prefix_v = pl.BlockSpec((prefix_rows, HD), lambda g: (0, g + HK))
    branch_k = pl.BlockSpec((num_blocks, block, HD), lambda g: (0, 0, g))
    branch_v = pl.BlockSpec((num_blocks, block, HD), lambda g: (0, 0, g + HK))
    grad_prefix = jax.ShapeDtypeStruct((prefix_rows, features // 2), F32)
    grad_branch = jax.ShapeDtypeStruct((num_blocks, block, features // 2), F32)
    out, d_query, dpk, dpv, dbk, dbv = pl.pallas_call(
        functools.partial(attend_kernel, slots),
        grid=(HK,),
        in_specs=[smem, smem, heads, heads, prefix_k, prefix_v, branch_k, branch_v],
        out_specs=[heads, heads, prefix_k, prefix_k, branch_k, branch_k],
        out_shape=[
            jax.ShapeDtypeStruct((block, width), BF16),
            jax.ShapeDtypeStruct((block, width), BF16),
            grad_prefix, grad_prefix, grad_branch, grad_branch,
        ],
        compiler_params=pltpu.CompilerParams(vmem_limit_bytes=56 * 1024 * 1024),
    )(parents, lengths, query[0], d_out[0], prefix_all, prefix_all, all_blocks, all_blocks)
    spread = jnp.concatenate([dbk, dbv], axis=2).reshape(num_blocks * block, features)
    grad_branch = lax.psum_scatter(spread, "ctx", scatter_dimension=0, tiled=True)
    grad_rows = lax.psum_scatter(jnp.concatenate([dpk, dpv], axis=1), "ctx", scatter_dimension=0, tiled=True)
    grad_prefix_out = lax.psum_scatter(grad_rows, "smp", scatter_dimension=1, tiled=True)
    return out[None], d_query[None], grad_branch.astype(BF16)[None], grad_prefix_out.astype(BF16)


SLOTS = 3
MESH = pl.DeviceIdType.MESH
VMEM_LIMIT = 56 * 1024 * 1024


def greet(ctx_size, smp_size, me, smp):
    barrier = pltpu.get_barrier_semaphore()
    for d in range(1, ctx_size):
        pl.semaphore_signal(barrier, inc=1, device_id={"ctx": lax.rem(me + d, ctx_size)}, device_id_type=MESH)
    for d in range(1, smp_size):
        pl.semaphore_signal(barrier, inc=1, device_id={"smp": lax.rem(smp + d, smp_size)}, device_id_type=MESH)
    pl.semaphore_wait(barrier, ctx_size + smp_size - 2)


def remote(src, dst, send, recv, to):
    return pltpu.make_async_remote_copy(
        src_ref=src, dst_ref=dst, send_sem=send, recv_sem=recv, device_id=to, device_id_type=MESH
    )


HEAD_ORDER = (0, 2, 1, 3)


def block_columns(i):
    return slice(i * HD, (i + 1) * HD)


def tree_kernel(
    ctx_size, smp_size, parents, lengths, query_far, d_out_far, branch, prefix,
    out_far, d_query_far, d_branch, d_prefix,
    query, d_out, out, d_query, load_sem, store_sem,
    own, held, stage, pre_own, pre, mine, d_own, other, sums, to_beside, below, other_in, beside_in,
    d_pre, p_in, p_sum, p_low, q_in,
    up_send, up_recv, over_send, over_recv, aside_send, aside_recv, a_send, a_recv, b_send, b_recv,
    down_send, down_recv, cross_send, cross_recv, back_send, back_recv, p_send, p_recv, q_send, q_recv,
):
    me, smp = lax.axis_index("ctx"), lax.axis_index("smp")
    side = lax.rem(me, 2)
    beside = me + 1 - 2 * side
    block = branch.shape[0]
    group_width = query.shape[1] // HK
    p_rows = prefix.shape[0]
    prefix_rows = pre.shape[1]
    loads = [
        pltpu.make_async_copy(query_far, query, load_sem.at[0]), pltpu.make_async_copy(d_out_far, d_out, load_sem.at[1])
    ]
    for load in loads:
        load.start()
    greet(ctx_size, smp_size, me, smp)

    def up(src, k, c):
        return remote(src, held.at[c, k, side], up_send.at[k, c], up_recv.at[k, c], {"ctx": me + 2})

    def aside(k, c):
        half = held.at[c, k, side]
        return remote(half, half, aside_send.at[k, c], aside_recv.at[k, c], {"ctx": beside})

    def over(k, c):
        return remote(own.at[c], held.at[c, k], over_send.at[c], over_recv.at[c], {"ctx": beside})

    def over_keys(k, c):
        return remote(own.at[c, 0], held.at[c, k, 0], over_send.at[c], over_recv.at[c], {"ctx": beside})

    def down(k, c):
        return remote(sums.at[c, k], below.at[c, k], down_send.at[k, c], down_recv.at[k, c], {"ctx": me - 2})

    def cross(k, c):
        return remote(other.at[c, k], other_in.at[c, k], cross_send.at[k, c], cross_recv.at[k, c], {"ctx": beside})

    def back(c):
        return remote(to_beside.at[c], beside_in.at[c], back_send.at[c], back_recv.at[c], {"ctx": beside})

    def back_keys(c):
        return remote(to_beside.at[c, 0], beside_in.at[c, 0], back_send.at[c], back_recv.at[c], {"ctx": beside})

    my_rows = pl.ds(pl.multiple_of(me * p_rows, p_rows), p_rows)
    my_columns = pl.ds(2 * smp, 2)

    def a_copy(d):
        return remote(
            pre_own, pre.at[my_columns, my_rows], a_send.at[d - 1], a_recv.at[d - 1], {"ctx": lax.rem(me + d, ctx_size)}
        )

    def b_copy(d, i):
        columns = pre.at[2 * smp + i]
        return remote(columns, columns, b_send.at[d - 1, i], b_recv.at[d - 1, i], {"smp": lax.rem(smp + d, smp_size)})

    def p_copy(to, d, i):
        return remote(
            d_pre.at[2 * to + i], p_in.at[d - 1, i], p_send.at[d - 1, i], p_recv.at[d - 1, i], {"smp": to}
        )

    def p_after(d, i):
        return p_copy(lax.rem(smp + d, smp_size), d, i)

    def head_columns(c):
        head = 2 * lax.rem(c, 2) + lax.div(c, 2)
        return pl.ds(pl.multiple_of(head * group_width, group_width), group_width)

    def stores(c):
        columns = head_columns(c)
        return [
            pltpu.make_async_copy(src.at[:, columns], dst.at[:, columns], store_sem.at[i, c])
            for i, (src, dst) in enumerate(((out, out_far), (d_query, d_query_far)))
        ]

    def q_copy(d):
        to = lax.rem(me + d, ctx_size)
        rows = pl.ds(pl.multiple_of(to * p_rows, p_rows), p_rows)
        return remote(p_low.at[:, rows], q_in.at[d - 1], q_send.at[d - 1], q_recv.at[d - 1], {"ctx": to})

    for i in range(2):
        pre_own[i] = prefix[:, i * HD:(i + 1) * HD]
        pre[2 * smp + i, my_rows] = prefix[:, i * HD:(i + 1) * HD]
    for d in range(1, ctx_size):
        a_copy(d).start()
    for c in range(HK):
        for i in range(2):
            own[c, i] = branch[:, block_columns(HK * i + HEAD_ORDER[c])]
    for device, k in ((0, 0), (1, 1), (2, 2), (4, 3), (5, 3), (6, 3)):
        @pl.when(me == device)
        def _():
            for c in range(2):
                (over_keys if device in (1, 5) else over)(k, c).start()
                if k < 3:
                    up(own.at[c, device % 2], k, c).start()
    for k, without in ((0, me == 0), (1, me < 2), (2, (me < 3) | (me > 5)), (3, (me < 5) | (me == 6))):
        @pl.when(without)
        def _():
            for c in range(HK):
                held[c, k, 1] = jnp.zeros((block, HD), BF16)
    for k, without in ((0, me == 0), (1, me == 1), (2, (me < 3) | (me > 5)), (3, (me < 4) | (me == 6))):
        @pl.when(without)
        def _():
            for c in range(HK):
                held[c, k, 0] = jnp.zeros((block, HD), BF16)
    for d in range(1, ctx_size):
        a_copy(d).wait_recv()
    for i in range(2):
        for d in range(1, smp_size):
            b_copy(d, i).start()

    first = parents[0, 6]
    second = jnp.where(first >= 0, parents[0, jnp.maximum(first, 0)], -1)
    found = walk_up(parents, lengths, me, SLOTS)
    weight = []
    for s, (index, _, there) in enumerate(found):
        place = jnp.where(me < 6, jnp.minimum(index, 3), jnp.where(me == 6, s, 3 if s == 0 else s - 1))
        weight.append([jnp.where(there & (place == k), 1.0, 0.0) for k in range(4)])

    def forward(c):
        def pass_on(k):
            up(held.at[c, k, side], k, c).wait_recv()
            up(held.at[c, k, side], k, c).start()
            aside(k, c).start()

        @pl.when(me == 0)
        def _():
            over_keys(1, c).wait_recv()
            up(held.at[c, 1, 0], 1, c).start()

        @pl.when(me == 1)
        def _():
            over(0, c).wait_recv()
            up(held.at[c, 0, 1], 0, c).start()

        @pl.when(me == 2)
        def _():
            pass_on(0)
            pass_on(1)

        @pl.when(me == 3)
        def _():
            over(2, c).wait_recv()
            up(held.at[c, 2, 1], 2, c).start()
            pass_on(1)
            pass_on(0)

        @pl.when((me == 4) | (me == 5))
        def _():
            for k in range(3):
                up(held.at[c, k, side], k, c).wait_recv()
                aside(k, c).start()

        @pl.when(me == 4)
        def _():
            over_keys(3, c).wait_recv()

        @pl.when(me == 5)
        def _():
            over(3, c).wait_recv()

        @pl.when((me == 4) | (me == 5))
        def _():
            for k, want in enumerate((first, second)):
                total = jnp.where(want == me, 1.0, 0.0) * own[c, side].astype(F32)
                for slot, index in ((0, 0), (1, 1), (2, 2), (3, beside)):
                    total += jnp.where(want == index, 1.0, 0.0) * held[c, slot, side].astype(F32)
                stage[c, k] = total.astype(BF16)
                up(stage.at[c, k], k, c).start()

        @pl.when(me >= 6)
        def _():
            for k in range(2):
                up(held.at[c, k, side], k, c).wait_recv()
                aside(k, c).start()

        @pl.when(me == 7)
        def _():
            over(3, c).wait_recv()

        for device, k in ((0, 0), (1, 1), (2, 2), (4, 3), (5, 3), (6, 3)):
            @pl.when((me == device) & (c < HK - 2))
            def _():
                (over_keys if device in (1, 5) else over)(k, c + 2).start()
                if k < 3:
                    up(own.at[c + 2, device % 2], k, c + 2).start()

    def settle(c):
        @pl.when(me >= 2)
        def _():
            for k in range(2):
                aside(k, c).wait_recv()

        @pl.when((me == 4) | (me == 5))
        def _():
            aside(2, c).wait_recv()

    def compute(c):
        sides = []
        head = 2 * lax.rem(c, 2) + lax.div(c, 2)
        for i in range(2):
            parts = [pre[HK * i + head], own[c, i]]
            slots = [held[c, k, i].astype(F32) for k in range(4)]
            for w in weight:
                parts.append((w[0] * slots[0] + w[1] * slots[1] + w[2] * slots[2] + w[3] * slots[3]).astype(BF16))
            sides.append(jnp.concatenate(parts, axis=0))
        columns = head_columns(c)
        out[:, columns], d_query[:, columns], grad_keys, grad_values = attend_group(
            query[:, columns], d_out[:, columns], sides[0], sides[1], prefix_rows, lengths[0, me],
            [length for _, length, _ in found],
        )
        for i, grads in enumerate((grad_keys, grad_values)):
            d_pre[HK * i + head] = grads[:prefix_rows].astype(BF16)
            d_own[c, i] = grads[prefix_rows:prefix_rows + block]
            pieces = [grads[prefix_rows + s * block:prefix_rows + (s + 1) * block] for s in range(1, SLOTS + 1)]
            for k in range(4):
                mine[c, k, i] = weight[0][k] * pieces[0] + weight[1][k] * pieces[1] + weight[2][k] * pieces[2]

        for store in stores(c):
            store.start()

        @pl.when(me >= 2)
        def _():
            for k in range(2):
                other[c, k] = mine[c, k, 1 - side].astype(BF16)
                cross(k, c).start()

        @pl.when((me == 4) | (me == 5))
        def _():
            other[c, 2] = mine[c, 2, 1 - side].astype(BF16)
            cross(2, c).start()

        @pl.when(me == 7)
        def _():
            to_beside[c] = mine[c, 3].astype(BF16)
            back(c).start()

        for i in range(2):
            to = 2 * i + lax.rem(c, 2)

            @pl.when(smp != to)
            def _():
                p_copy(to, lax.rem(to - smp + 4, 4), lax.div(c, 2)).start()

    def shared(c, index):
        near, far = below[c, 0].astype(F32), below[c, 1].astype(F32)
        return jnp.where(first == index, 1.0, 0.0) * near + jnp.where(second == index, 1.0, 0.0) * far

    def add_down(c):
        def send_sum(k, more):
            cross(k, c).wait_recv()
            total = mine[c, k, side] + other_in[c, k].astype(F32)
            if more is not None:
                total += more
            sums[c, k] = total.astype(BF16)
            down(k, c).start()

        @pl.when(me >= 6)
        def _():
            for k in range(2):
                send_sum(k, None)

        @pl.when((me == 4) | (me == 5))
        def _():
            for k in range(2):
                down(k, c).wait_recv()
            for k in range(3):
                send_sum(k, shared(c, k))

        @pl.when(me == 4)
        def _():
            to_beside[c, 0] = (mine[c, 3, 0] + shared(c, 5)).astype(BF16)
            back_keys(c).start()

        @pl.when(me == 5)
        def _():
            to_beside[c, 0] = mine[c, 3, 0].astype(BF16)
            to_beside[c, 1] = (mine[c, 3, 1] + shared(c, 4)).astype(BF16)
            back(c).start()

        @pl.when((me == 2) | (me == 3))
        def _():
            for k in range(2):
                down(k, c).wait_recv()
                send_sum(k, below[c, k].astype(F32))
            down(2, c).wait_recv()

        @pl.when(me == 3)
        def _():
            to_beside[c, 0] = mine[c, 2, 0].astype(BF16)
            to_beside[c, 1] = (mine[c, 2, 1] + below[c, 2].astype(F32)).astype(BF16)
            back(c).start()

        @pl.when(me < 2)
        def _():
            for k in range(2):
                down(k, c).wait_recv()

        @pl.when(me == 0)
        def _():
            to_beside[c, 0] = (mine[c, 1, 0] + below[c, 1].astype(F32)).astype(BF16)
            back_keys(c).start()

        @pl.when(me == 1)
        def _():
            to_beside[c, 0] = mine[c, 0, 0].astype(BF16)
            to_beside[c, 1] = (mine[c, 0, 1] + below[c, 0].astype(F32)).astype(BF16)
            back(c).start()

    def sum_prefix():
        for d in range(1, smp_size):
            for i in range(2):
                p_after(d, i).wait_recv()
        total = d_pre[my_columns].astype(F32)
        for d in range(1, smp_size):
            total += p_in[d - 1].astype(F32)
        p_sum[...] = total
        p_low[...] = total.astype(BF16)
        for d in range(1, ctx_size):
            q_copy(d).start()

    down_lag = jnp.where(me >= 6, 2, jnp.where(me >= 4, 3, 4))
    prefix_step = jnp.where((me >= 4) & (me < 6), HK + 2, HK + 1)

    @pl.loop(0, 2 * HK)
    def _(t):
        @pl.when(t < HK)
        def _():
            forward(t)

        @pl.when(t == 1)
        def _():
            for load in loads:
                load.wait()
            for d in range(1, smp_size):
                b_copy(d, 0).wait_recv()

        @pl.when(t == 3)
        def _():
            for d in range(1, smp_size):
                b_copy(d, 1).wait_recv()

        @pl.when((t >= 1) & (t < HK + 1))
        def _():
            settle(t - 1)
            compute(t - 1)

        @pl.when((t >= down_lag) & (t < HK + down_lag))
        def _():
            add_down(t - down_lag)

        @pl.when(t == prefix_step)
        def _():
            sum_prefix()

    for device in (0, 1, 2, 4, 5, 6):
        @pl.when(me == device)
        def _():
            for c in range(HK):
                if device in (1, 5):
                    back_keys(c).wait_recv()
                else:
                    back(c).wait_recv()
                for i in range(2):
                    total = d_own[c, i]
                    if i == 0 or device not in (1, 5):
                        total += beside_in[c, i].astype(F32)
                    if i == device % 2 and device < 3:
                        total += below[c, device].astype(F32)
                    elif i == device % 2 and device < 6:
                        total += shared(c, device)
                    d_branch[:, block_columns(HK * i + HEAD_ORDER[c])] = total.astype(BF16)

    @pl.when((me == 3) | (me == 7))
    def _():
        for c in range(HK):
            for i in range(2):
                d_branch[:, block_columns(HK * i + HEAD_ORDER[c])] = d_own[c, i].astype(BF16)

    total = p_sum[:, my_rows]
    for d in range(1, ctx_size):
        q_copy(d).wait_recv()
        total += q_in[d - 1].astype(F32)
    for i in range(2):
        d_prefix[:, i * HD:(i + 1) * HD] = total[i].astype(BF16)

    for d in range(1, ctx_size):
        a_copy(d).wait_send()
        q_copy(d).wait_send()
    for d in range(1, smp_size):
        for i in range(2):
            b_copy(d, i).wait_send()
            p_after(d, i).wait_send()
    for c in range(HK):
        for store in stores(c):
            store.wait()

    def drain(active, copies):
        @pl.when(active)
        def _():
            for c in range(HK):
                for copy in copies:
                    copy(c).wait_send()

    def on(copy, k):
        return lambda c: copy(k, c)

    def climb(k):
        return lambda c: up(stage.at[c, 0], k, c)

    even = (me == 0) | (me == 2) | (me == 4) | (me == 6)
    drain(even, (on(over, 0),))
    drain((me == 1) | (me == 5), (on(over_keys, 1),))
    drain(me < 6, (climb(0), climb(1)))
    drain((me == 2) | (me == 3), (climb(2),))
    drain(me >= 2, (on(aside, 0), on(aside, 1), on(cross, 0), on(cross, 1), on(down, 0), on(down, 1)))
    drain((me == 4) | (me == 5), (on(aside, 2), on(cross, 2), on(down, 2)))
    drain(side == 1, (back,))
    drain((me == 0) | (me == 4), (back_keys,))


def hand_over_kernel(a, b, c, d, a_out, b_out, c_out, d_out):
    for src, dst in ((a, a_out), (b, b_out), (c, c_out), (d, d_out)):
        dst[...] = src[...]


def per_device(query, d_out, branch_kv, prefix_kv, parents, lengths):
    ctx_size, smp_size = lax.axis_size("ctx"), lax.axis_size("smp")
    p_rows, p_cols = prefix_kv.shape
    if parents.shape[1] != 8 or ctx_size != 8 or p_cols != 2 * HD or smp_size != 4:
        return per_device_general(query, d_out, branch_kv, prefix_kv, parents, lengths)
    block, width = query.shape[1:]
    prefix_rows = p_rows * ctx_size
    smem = pl.BlockSpec(memory_space=pltpu.SMEM)
    vmem = pl.BlockSpec(memory_space=pltpu.VMEM)
    dma = pltpu.SemaphoreType.DMA
    anywhere = pl.BlockSpec(memory_space=pl.ANY)
    half = (block, HD)
    pair = (2,) + half
    results = pl.pallas_call(
        functools.partial(tree_kernel, ctx_size, smp_size),
        in_specs=[smem, smem, anywhere, anywhere, vmem, vmem],
        out_specs=[anywhere, anywhere, vmem, vmem],
        out_shape=[
            jax.ShapeDtypeStruct((block, width), BF16),
            jax.ShapeDtypeStruct((block, width), BF16),
            jax.ShapeDtypeStruct(branch_kv.shape[1:], BF16),
            jax.ShapeDtypeStruct(prefix_kv.shape, BF16),
        ],
        scratch_shapes=[
            pltpu.VMEM((block, width), BF16),
            pltpu.VMEM((block, width), BF16),
            pltpu.VMEM((block, width), BF16),
            pltpu.VMEM((block, width), BF16),
            dma((2,)), dma((2, HK)),
            pltpu.VMEM((HK,) + pair, BF16),
            pltpu.VMEM((HK, 4) + pair, BF16),
            pltpu.VMEM((HK, 2) + half, BF16),
            pltpu.VMEM((2, p_rows, HD), BF16),
            pltpu.VMEM((2 * HK, prefix_rows, HD), BF16),
            pltpu.VMEM((HK, 4) + pair, F32),
            pltpu.VMEM((HK,) + pair, F32),
            pltpu.VMEM((HK, 3) + half, BF16),
            pltpu.VMEM((HK, 3) + half, BF16),
            pltpu.VMEM((HK,) + pair, BF16),
            pltpu.VMEM((HK, 3) + half, BF16),
            pltpu.VMEM((HK, 3) + half, BF16),
            pltpu.VMEM((HK,) + pair, BF16),
            pltpu.VMEM((2 * HK, prefix_rows, HD), BF16),
            pltpu.VMEM((smp_size - 1, 2, prefix_rows, HD), BF16),
            pltpu.VMEM((2, prefix_rows, HD), F32),
            pltpu.VMEM((2, prefix_rows, HD), BF16),
            pltpu.VMEM((ctx_size - 1, 2, p_rows, HD), BF16),
            dma((3, HK)), dma((3, HK)), dma((HK,)), dma((HK,)), dma((3, HK)), dma((3, HK)),
            dma((ctx_size - 1,)), dma((ctx_size - 1,)), dma((smp_size - 1, 2)), dma((smp_size - 1, 2)),
            dma((3, HK)), dma((3, HK)), dma((3, HK)), dma((3, HK)), dma((HK,)), dma((HK,)),
            dma((smp_size - 1, 2)), dma((smp_size - 1, 2)), dma((ctx_size - 1,)), dma((ctx_size - 1,)),
        ],
        compiler_params=pltpu.CompilerParams(
            collective_id=0, has_side_effects=True, vmem_limit_bytes=VMEM_LIMIT
        ),
        name="tree_attention",
    )(parents, lengths, query[0], d_out[0], branch_kv[0], prefix_kv)
    rows = [pl.BlockSpec((x.shape[0] // 2, x.shape[1]), lambda r: (r, 0)) for x in results[:3]]
    rows.append(pl.BlockSpec(results[3].shape, lambda r: (0, 0)))
    out, d_query, d_branch, d_prefix = pl.pallas_call(
        hand_over_kernel,
        grid=(2,),
        in_specs=rows,
        out_specs=rows,
        out_shape=[jax.ShapeDtypeStruct(x.shape, x.dtype) for x in results],
        name="hand_over",
    )(*results)
    return out[None], d_query[None], d_branch[None], d_prefix


def solution(mesh):
    return jax.shard_map(
        per_device,
        mesh=mesh,
        in_specs=(
            P("smp", "ctx", None),
            P("smp", "ctx", None),
            P("smp", "ctx", None),
            P("ctx", "smp"),
            P("smp", None),
            P("smp", None),
        ),
        out_specs=(
            P("smp", "ctx", None),
            P("smp", "ctx", None),
            P("smp", "ctx", None),
            P("ctx", "smp"),
        ),
        check_vma=False,
    )
```
